512 devices in a mesh: tm: 16 (over z_hi, y, core), row: 4 (over x), col: 8 (over z_lo).
Axes of the slice: x: 4, y: 4, z: 16 (z_hi: 2, z_lo: 8; z = z_hi * 8 + z_lo), core: 2. Of those that a mesh axis runs over, the one named last changes fastest.
Arguments:
- particles: float32 [16, 8192, 256], P('tm', ('row', 'col')), may hold values from -6 to 6
- source_pots: float32 [16, 8192], P('tm', ('row', 'col')), may hold values from 0.85 to 1.15
- target_pots: float32 [16, 8192], P('tm', ('row', 'col')), may hold values from 0.85 to 1.15
Outputs:
- gradient: float32 [16, 8192, 256], P('tm', ('row', 'col'))
The draws below stay inside these ranges and needn't reach their ends.
All inputs are finite; a program needn't handle non-finite values.
Results may differ from the reference program's by a relative error of at most 0.0003.
Values sent between devices are 32-bit elements; how exact they have to be, the bound alone decides.
A program may use at most 64 MiB of HBM per device.

```python
import jax
import jax.numpy as jnp
from jax import lax

D = 256
TIMES = 16
PARTICLES = 8192


def block_scale(rng, dims, pieces, low, high):
    factor_of = 1.0
    for dim, blocks in pieces:
        heights = jax.random.uniform(jax.random.fold_in(jax.random.fold_in(rng, 6), dim), (blocks,), jnp.float32, low / len(pieces), high / len(pieces))
        factor_of = factor_of * jnp.repeat(jnp.exp(heights), dims[dim] // blocks).reshape((-1,) + (1,) * (len(dims) - 1 - dim))
    return factor_of


def normal_values(stream_key, shape, width, bound, pieces=(), kind=jnp.bfloat16):
    result = jax.random.normal(stream_key, shape, jnp.float32) * width
    if len(pieces) > 0:
        result = block_scale(stream_key, shape, pieces, -0.22, 0.18) * result
    return jnp.clip(result, min=-bound, max=bound).astype(kind)


def setup_inputs(seed: int = 0) -> dict:
    splits = jax.random.split(jax.random.key(seed), 4)
    particles = normal_values(splits[0], (TIMES, PARTICLES, D), 1.0, 6.0, ((0, 16), (1, 32)), jnp.float32)
    source_pots = jnp.clip(0.85 + 0.29999995 * jax.random.uniform(splits[1], (TIMES, PARTICLES), jnp.float32) ** block_scale(splits[1], (TIMES, PARTICLES), ((0, 16), (1, 32)), -0.2, 0.2), 0.85, 1.15)
    target_pots = jnp.clip(0.85 + 0.29999995 * jax.random.uniform(splits[2], (TIMES, PARTICLES), jnp.float32) ** block_scale(splits[2], (TIMES, PARTICLES), ((0, 16), (1, 32)), -0.2, 0.2), 0.85, 1.15)
    return {"particles": particles, "source_pots": source_pots, "target_pots": target_pots}


EPS = 0.1


def tile_terms(row_points, row_pots, col_points, col_pots, population):
    features = row_points.shape[1]
    row_norms = jnp.sum(row_points * row_points, axis=1)
    col_norms = jnp.sum(col_points * col_points, axis=1)
    crossed = lax.dot_general(row_points, col_points, (((1,), (1,)), ((), ())), precision=lax.Precision.HIGHEST, preferred_element_type=jnp.float32)
    distance = (row_norms[:, None] + col_norms[None, :] - 2.0 * crossed) / features
    weights = jnp.exp((row_pots[:, None] + col_pots[None, :] - distance) / EPS) / population
    source = jnp.sum(weights, axis=1)[:, None] * row_points - jnp.dot(weights, col_points, precision=lax.Precision.HIGHEST, preferred_element_type=jnp.float32)
    target = jnp.sum(weights, axis=0)[:, None] * col_points - lax.dot_general(weights, row_points, (((0,), (0,)), ((), ())), precision=lax.Precision.HIGHEST, preferred_element_type=jnp.float32)
    return source, target


def reference(particles, source_pots, target_pots):
    horizon, population, features = particles.shape
    row_block = min(1024, population)
    blocks_n = population // row_block

    def transport(sources, source_vals, targets, target_vals):
        source_blocks = sources.reshape(blocks_n, row_block, features)
        value_blocks = source_vals.reshape(blocks_n, row_block)

        def advance(running, element):
            source, target = tile_terms(element[0], element[1], targets, target_vals, population)
            return running + target, source

        target_sum, source_rows = lax.scan(advance, jnp.zeros((population, features), jnp.float32), (source_blocks, value_blocks))
        return source_rows.reshape(population, features), target_sum

    gradients = [jnp.zeros((population, features), jnp.float32) for moment in range(horizon)]
    for moment in range(horizon - 1):
        source, target = transport(particles[moment], source_pots[moment], particles[moment + 1], target_pots[moment + 1])
        gradients[moment] = gradients[moment] + source
        gradients[moment + 1] = gradients[moment + 1] + target
    return jnp.stack(gradients)
```

```python
import functools
import math

import jax
import jax.numpy as jnp
from jax import lax
from jax.experimental import pallas as pl
from jax.experimental.pallas import tpu as pltpu
from jax.sharding import PartitionSpec as P

EPS = 0.1
MESH = pl.DeviceIdType.MESH
F32 = jnp.float32
BF16 = jnp.bfloat16


def split(x):
    hi = x.astype(BF16)
    return hi, (x - hi.astype(F32)).astype(BF16)


def dot(a, b, dims):
    return lax.dot_general(a, b, (dims, ((), ())), preferred_element_type=F32)


def dot3(a, b, dims):
    return dot(a[0], b[0], dims) + dot(a[0], b[1], dims) + dot(a[1], b[0], dims)


def eye(n):
    return lax.broadcasted_iota(jnp.int32, (n, n), 0) == lax.broadcasted_iota(jnp.int32, (n, n), 1)


def to_row(col):
    n = col.shape[0]
    return jnp.sum(jnp.where(eye(n), col, 0.0), axis=0, keepdims=True)


def to_col(row):
    n = row.shape[1]
    return jnp.sum(jnp.where(eye(n), row, 0.0), axis=1, keepdims=True)


def kernel(
    dims,
    pts_ref,
    spot_ref,
    tpot_ref,
    out_ref,
    sbuf,
    mbuf,
    mhi,
    mlo,
    brow,
    part,
    sib_part,
    right_sum,
    left_sum,
    gmt,
    csum,
    gm,
    gm_in,
    gtm_in,
    fin,
    zr_s,
    zr_r,
    zl_s,
    zl_r,
    sib_s,
    sib_r,
    own_s,
    own_r,
    tm_s,
    tm_r,
    mx_s,
    mx_r,
    pe_s,
    pe_r,
    cr_s,
    cr_r,
    cl_s,
    cl_r,
    gm_s,
    gm_r,
    gt_s,
    gt_r,
    fin_s,
    fin_r,
):
    times, nx, nz, rows, feats = dims
    half = rows // 2
    hrow = half + 8
    last = nz - 1
    population = rows * nx * nz
    scale = math.log2(math.e) / EPS
    tm, x, z = lax.axis_index("tm"), lax.axis_index("row"), lax.axis_index("col")
    core = lax.rem(tm, 2)
    is0, is1 = core == 0, core == 1
    active = tm < times - 1
    fed = jnp.logical_and(is1, active)
    feeds = jnp.logical_and(is0, tm > 0)
    has_left, has_right = z > 0, z < last
    sib = (tm + 1 - 2 * core, x, z)
    zright, zleft = (tm, x, jnp.minimum(z + 1, last)), (tm, x, jnp.maximum(z - 1, 0))
    before, after = (jnp.maximum(tm - 1, 0), x, z), (jnp.minimum(tm + 1, times - 1), x, z)
    xs = [(tm, lax.rem(x + 1 + k, nx), z) for k in range(nx - 1)]

    def rdma(src, dst, s, r, to):
        return pltpu.make_async_remote_copy(
            src_ref=src, dst_ref=dst, send_sem=s, recv_sem=r, device_id=to, device_id_type=MESH
        )

    barrier = pltpu.get_barrier_semaphore()

    def greet(to):
        pl.semaphore_signal(barrier, inc=1, device_id=to, device_id_type=MESH)

    greet(sib)
    for to in xs:
        greet(to)
    pl.when(has_left)(lambda: greet(zleft))
    pl.when(has_right)(lambda: greet(zright))
    pl.when(feeds)(lambda: greet(before))
    pl.when(fed)(lambda: greet(after))

    pts = pts_ref[...]
    norm = to_row(jnp.sum(pts * pts, axis=1, keepdims=True)) * (scale / feats)
    trow = tpot_ref[...] * scale - norm
    srow = spot_ref[...] * scale - norm - math.log2(population)

    def put(buf, b):
        for h in range(2):
            buf[b, h * hrow : h * hrow + half, :] = pts[h * half : (h + 1) * half]
            pair = jnp.concatenate(
                [trow[:, h * half : (h + 1) * half], srow[:, h * half : (h + 1) * half], jnp.zeros((6, half), F32)], axis=0
            )
            buf[b, h * hrow + half : (h + 1) * hrow, :] = jnp.concatenate(
                [pair, jnp.zeros((8, feats - half), F32)], axis=1
            )

    pl.when(is0)(lambda: put(mbuf, x))
    pl.when(is1)(lambda: put(sbuf, z))
    gmt[...] = jnp.zeros_like(gmt)
    csum[...] = jnp.zeros_like(csum)

    partners = nx + has_left.astype(jnp.int32) + has_right.astype(jnp.int32)
    partners = partners + feeds.astype(jnp.int32) + fed.astype(jnp.int32)
    pl.semaphore_wait(barrier, partners)

    mine = pl.ds(pl.multiple_of(core * hrow, 8), hrow)
    other = pl.ds(pl.multiple_of((1 - core) * hrow, 8), hrow)

    def own_copy(h):
        ref = sbuf.at[z, pl.ds(h * hrow, hrow)]
        return rdma(ref, ref, own_s.at[h], own_r.at[h], sib)

    def tm_copy():
        return rdma(mbuf.at[x], mbuf.at[x], tm_s, tm_r, before)

    def mx_copy(k):
        return rdma(mbuf.at[x], mbuf.at[x], mx_s.at[k], mx_r.at[k], xs[k])

    def mx_arrival(k):
        ref = mbuf.at[lax.rem(x + nx - 1 - k, nx)]
        return rdma(ref, ref, mx_s.at[k], mx_r.at[k], xs[k])

    @pl.when(is1)
    def _():
        own_copy(0).start()
        own_copy(1).start()

    @pl.when(is0)
    def _():
        pl.when(feeds)(lambda: tm_copy().start())
        for k in range(nx - 1):
            mx_copy(k).start()
        own_copy(0).wait_recv()

    def zr_copy(s, b):
        ref = sbuf.at[b, mine]
        return rdma(ref, ref, zr_s.at[s], zr_r.at[s], zright)

    def zl_copy(s, b):
        ref = sbuf.at[b, mine]
        return rdma(ref, ref, zl_s.at[s], zl_r.at[s], zleft)

    def sib_copy(b, window):
        ref = sbuf.at[b, window]
        return rdma(ref, ref, sib_s.at[b], sib_r.at[b], sib)

    cross = tm == times // 2 - 1
    wait_m = jnp.where(cross, nz, 1)
    first = jnp.where(is0, 2, wait_m + 1)

    def order(n):
        low = jnp.minimum(z, last - z)
        d = (n + 1) // 2
        near = z + jnp.where(lax.rem(n, 2) == 1, -d, d)
        far = jnp.where(z < nz - nz // 2, n, last - n)
        return jnp.where(n <= 2 * low, near, far)

    mine_rows = pl.ds(pl.multiple_of(core * half, 8), half)
    other_rows = pl.ds(pl.multiple_of((1 - core) * half, 8), half)

    def pe_copy(b, window):
        return rdma(part.at[b, window], sib_part.at[b], pe_s.at[b], pe_r.at[b], sib)

    def prepare():
        for k in range(nx - 1):
            mx_arrival(k).wait_recv()
        for j in range(nx):
            for h in range(2):
                at = j * rows + h * half
                hi, lo = split(mbuf[j, h * hrow : h * hrow + half, :])
                mhi[at : at + half, :] = hi
                mlo[at : at + half, :] = lo
                pair = mbuf[j, h * hrow + half : (h + 1) * hrow, 0:half]
                brow[0:1, at : at + half] = jnp.where(is0, pair[1:2], pair[0:1])

    def tile(b):
        pieces, cols = [], []
        for h in range(2):
            pieces.append(sbuf[b, h * hrow : h * hrow + half, :])
            pair = sbuf[b, h * hrow + half : (h + 1) * hrow, 0:half]
            cols.append(to_col(jnp.where(is0, pair[0:1], pair[1:2])))
        s = jnp.concatenate(pieces, axis=0)
        acol = jnp.concatenate(cols, axis=0)
        ss = split(s)
        st = split(s.T)
        total = jnp.zeros((rows, 1), F32)
        moved = jnp.zeros((rows, feats), F32)
        for j in range(nx):
            at = slice(j * rows, (j + 1) * rows)
            m = (mhi[at, :], mlo[at, :])
            g = dot3(ss, m, ((1,), (1,)))
            w = jnp.exp2(g * (2.0 * scale / feats) + acol + brow[0:1, at])
            total = total + jnp.sum(w, axis=1, keepdims=True)
            csum[0:1, at] += jnp.sum(w, axis=0, keepdims=True)
            ww = split(w)
            moved = moved + dot3(ww, m, ((1,), (0,)))
            gmt[:, at] += dot3(st, ww, ((1,), (0,)))
        part[b] = total * s - moved

    def step(s, carry):
        @pl.when(jnp.logical_and(s >= 1, s <= last))
        def _():
            b = z - s

            @pl.when(b >= 0)
            def _():
                zr_copy(s - 1, b).wait_recv()

                @pl.when(jnp.logical_and(has_right, s < last))
                def _():
                    zr_copy(s, b).start()

                sib_copy(b, mine).start()

            c = z + s

            @pl.when(c <= last)
            def _():
                zl_copy(s - 1, c).wait_recv()

                @pl.when(jnp.logical_and(has_left, s < last))
                def _():
                    zl_copy(s, c).start()

                sib_copy(c, mine).start()

        @pl.when(s == 0)
        def _():
            pl.when(has_right)(lambda: zr_copy(0, z).start())
            pl.when(has_left)(lambda: zl_copy(0, z).start())

        @pl.when(jnp.logical_and(fed, s == wait_m))
        def _():
            ref = mbuf.at[x]
            rdma(ref, ref, tm_s, tm_r, before).wait_recv()
            for k in range(nx - 1):
                mx_copy(k).start()

        pl.when(jnp.logical_and(active, s == first))(prepare)

        n = s - first

        @pl.when(jnp.logical_and(n >= 0, n < nz))
        def _():
            b = order(n)

            @pl.when(b != z)
            def _():
                sib_copy(b, other).wait_recv()

            @pl.when(jnp.logical_and(b == z, is0))
            def _():
                own_copy(1).wait_recv()

            pl.when(active)(lambda: tile(b))

            @pl.when(jnp.logical_not(active))
            def _():
                part[b] = jnp.zeros((rows, feats), F32)

            pe_copy(b, other_rows).start()

        return carry

    lax.fori_loop(0, 2 * nz + 1, step, 0)

    def gm_copy(k):
        j = lax.rem(x + 1 + k, nx)
        return rdma(gm.at[j], gm_in.at[k], gm_s.at[k], gm_r.at[k], xs[k])

    @pl.when(active)
    def _():
        for j in range(nx):
            at = slice(j * rows, (j + 1) * rows)
            ccol = to_col(csum[0:1, at])
            g = gmt[:, at].T
            for h in range(2):
                lo = h * half
                gm[j, lo : lo + half, :] = (
                    ccol[lo : lo + half] * mbuf[j, h * hrow : h * hrow + half, :] - g[lo : lo + half]
                )
        for k in range(nx - 1):
            gm_copy(k).start()

    def cr_copy(b):
        return rdma(right_sum.at[b], right_sum.at[b], cr_s.at[b], cr_r.at[b], zright)

    def cl_copy(b):
        return rdma(left_sum.at[b], left_sum.at[b], cl_s.at[b], cl_r.at[b], zleft)

    for b in range(nz):
        pe_copy(b, mine_rows).wait_recv()

    def chain(s, carry):
        @pl.when(jnp.logical_and(has_right, s >= z))
        def _():
            b = last - s + z

            @pl.when(has_left)
            def _():
                cr_copy(b).wait_recv()
                right_sum[b] = right_sum[b] + part[b, mine_rows, :] + sib_part[b]

            @pl.when(jnp.logical_not(has_left))
            def _():
                right_sum[b] = part[b, mine_rows, :] + sib_part[b]

            cr_copy(b).start()

        @pl.when(jnp.logical_and(has_left, s >= last - z))
        def _():
            b = s + z - last

            @pl.when(has_right)
            def _():
                cl_copy(b).wait_recv()
                left_sum[b] = left_sum[b] + part[b, mine_rows, :] + sib_part[b]

            @pl.when(jnp.logical_not(has_right))
            def _():
                left_sum[b] = part[b, mine_rows, :] + sib_part[b]

            cl_copy(b).start()

        @pl.when(jnp.logical_and(active, s == 1))
        def _():
            total = gm[x]
            for k in range(nx - 1):
                gm_copy(k).wait_recv()
                total = total + gm_in[k]
            gm[x] = total

            @pl.when(is1)
            def _():
                rdma(gm.at[x], gtm_in, gt_s, gt_r, after).start()

        return carry

    lax.fori_loop(0, last, chain, 0)

    mine_sum = part[z, mine_rows, :] + sib_part[z]
    fin[0] = mine_sum

    @pl.when(has_left)
    def _():
        cr_copy(z).wait_recv()
        fin[0] = fin[0] + right_sum[z]

    @pl.when(has_right)
    def _():
        cl_copy(z).wait_recv()
        fin[0] = fin[0] + left_sum[z]

    fin_copy = rdma(fin.at[0], fin.at[1], fin_s, fin_r, sib)
    gt_copy = rdma(gm.at[x], gtm_in, gt_s, gt_r, after)

    @pl.when(is0)
    def _():
        fin_copy.start()
        out_ref[...] = gm[x]

        @pl.when(feeds)
        def _():
            gt_copy.wait_recv()
            out_ref[...] = out_ref[...] + gtm_in[...]

    @pl.when(is1)
    def _():
        out_ref[half:, :] = fin[0]
        fin_copy.wait_recv()
        out_ref[0:half, :] = fin[1]

    @pl.when(is1)
    def _():
        own_copy(0).wait_send()
        own_copy(1).wait_send()

    pl.when(is0)(lambda: fin_copy.wait_send())
    pl.when(feeds)(lambda: tm_copy().wait_send())
    pl.when(fed)(lambda: gt_copy.wait_send())

    @pl.when(active)
    def _():
        for k in range(nx - 1):
            mx_copy(k).wait_send()
            gm_copy(k).wait_send()

    def drain(b, carry):
        pe_copy(b, other_rows).wait_send()

        @pl.when(b != z)
        def _():
            sib_copy(b, mine).wait_send()

        @pl.when(jnp.logical_and(has_right, b <= z))
        def _():
            zr_copy(z - b, b).wait_send()

        @pl.when(jnp.logical_and(has_left, b >= z))
        def _():
            zl_copy(b - z, b).wait_send()

        pl.when(jnp.logical_and(has_right, b > z))(lambda: cr_copy(b).wait_send())
        pl.when(jnp.logical_and(has_left, b < z))(lambda: cl_copy(b).wait_send())
        return carry

    lax.fori_loop(0, nz, drain, 0)


def local(dims, particles, source_pots, target_pots):
    times, nx, nz, rows, feats = dims
    half = rows // 2
    dma = pltpu.SemaphoreType.DMA
    scratch = [
        pltpu.VMEM((nz, rows + 16, feats), F32),
        pltpu.VMEM((nx, rows + 16, feats), F32),
        pltpu.VMEM((nx * rows, feats), BF16),
        pltpu.VMEM((nx * rows, feats), BF16),
        pltpu.VMEM((8, nx * rows), F32),
        pltpu.VMEM((nz, rows, feats), F32),
        pltpu.VMEM((nz, half, feats), F32),
        pltpu.VMEM((nz, half, feats), F32),
        pltpu.VMEM((nz, half, feats), F32),
        pltpu.VMEM((feats, nx * rows), F32),
        pltpu.VMEM((8, nx * rows), F32),
        pltpu.VMEM((nx, rows, feats), F32),
        pltpu.VMEM((nx - 1, rows, feats), F32),
        pltpu.VMEM((rows, feats), F32),
        pltpu.VMEM((2, half, feats), F32),
    ]
    for count in (nz, nz, nz, 2, 0, nx - 1, nz, nz, nz, nx - 1, 0, 0):
        kind = dma((count,)) if count else dma
        scratch += [kind, kind]
    out = pl.pallas_call(
        functools.partial(kernel, dims),
        out_shape=jax.ShapeDtypeStruct((rows, feats), F32),
        in_specs=[pl.BlockSpec(memory_space=pltpu.VMEM)] * 3,
        out_specs=pl.BlockSpec(memory_space=pltpu.VMEM),
        scratch_shapes=scratch,
        compiler_params=pltpu.CompilerParams(
            collective_id=0, has_side_effects=True, vmem_limit_bytes=56 * 2**20
        ),
    )(particles[0], source_pots, target_pots)
    return out[None]


def solution(mesh):
    times, nx, nz = mesh.shape["tm"], mesh.shape["row"], mesh.shape["col"]

    def program(particles, source_pots, target_pots):
        rows = particles.shape[1] // (nx * nz)
        dims = (times, nx, nz, rows, particles.shape[2])
        return jax.shard_map(
            functools.partial(local, dims),
            mesh=mesh,
            in_specs=(P("tm", ("row", "col"), None), P("tm", ("row", "col")), P("tm", ("row", "col"))),
            out_specs=P("tm", ("row", "col"), None),
            check_vma=False,
        )(particles, source_pots, target_pots)

    return program
```

```python
import functools
import math

import jax
import jax.numpy as jnp
from jax import lax
from jax.experimental import pallas as pl
from jax.experimental.pallas import tpu as pltpu
from jax.sharding import PartitionSpec as P

EPS = 0.1
MESH = pl.DeviceIdType.MESH
F32 = jnp.float32
BF16 = jnp.bfloat16


def split(x):
    hi = x.astype(BF16)
    return hi, (x - hi.astype(F32)).astype(BF16)


def dot(a, b, dims):
    return lax.dot_general(a, b, (dims, ((), ())), preferred_element_type=F32)


def dot3(a, b, dims):
    return dot(a[0], b[0], dims) + dot(a[0], b[1], dims) + dot(a[1], b[0], dims)


def eye(n):
    return lax.broadcasted_iota(jnp.int32, (n, n), 0) == lax.broadcasted_iota(jnp.int32, (n, n), 1)


def to_row(col):
    n = col.shape[0]
    return jnp.sum(jnp.where(eye(n), col, 0.0), axis=0, keepdims=True)


def to_col(row):
    n = row.shape[1]
    return jnp.sum(jnp.where(eye(n), row, 0.0), axis=1, keepdims=True)


BUFS = (
    "sbuf", "mbuf", "mhi", "mlo", "brow", "part", "sib_part", "rsum", "lsum", "gmt", "csum", "gm",
    "gx_in", "gmid", "gtm_in", "fin", "relay", "back", "shi", "slo", "thi", "tlo", "acol",
)
SEMS = (
    "own", "zr", "zl", "sib", "tm", "mx", "pe", "cr", "cl", "gx", "gt", "fi",
    "fx", "bx",
)
CH = 2


def kernel(dims, pts_ref, spot_ref, tpot_ref, out_ref, *scratch):
    times, nx, nz, rows, feats = dims
    half = rows // 2
    hrow = half + 8
    piece = half // CH
    last = nz - 1
    mid = times // 2
    spread = mid // 2
    population = rows * nx * nz
    scale = math.log2(math.e) / EPS
    v = dict(zip(BUFS, scratch))
    sems = {name: scratch[len(BUFS) + 2 * i : len(BUFS) + 2 * i + 2] for i, name in enumerate(SEMS)}
    sbuf, mbuf, part, gm, fin = v["sbuf"], v["mbuf"], v["part"], v["gm"], v["fin"]
    mhi, mlo, brow, gmt, csum = v["mhi"], v["mlo"], v["brow"], v["gmt"], v["csum"]
    gx_in = v["gx_in"]

    tm, x, z = lax.axis_index("tm"), lax.axis_index("row"), lax.axis_index("col")
    core = lax.rem(tm, 2)
    is0, is1 = core == 0, core == 1
    active = tm < times - 1
    cross = tm == mid - 1
    crossed = tm == mid
    fed = jnp.logical_and(jnp.logical_and(is1, active), jnp.logical_not(cross))
    feeds = jnp.logical_and(jnp.logical_and(is0, tm > 0), jnp.logical_not(crossed))
    has_left, has_right = z > 0, z < last
    sib = (tm + 1 - 2 * core, x, z)
    zright, zleft = (tm, x, jnp.minimum(z + 1, last)), (tm, x, jnp.maximum(z - 1, 0))
    before, after = (jnp.maximum(tm - 1, 0), x, z), (jnp.minimum(tm + 1, times - 1), x, z)
    x1, x2, x3 = lax.rem(x + 1, nx), lax.rem(x + 2, nx), lax.rem(x + 3, nx)
    xright, xleft = (tm, x1, z), (tm, x3, z)

    def at_time(t):
        return (t, x, z)

    def rdma(src, dst, name, to, k=None):
        s, r = sems[name]
        if k is not None:
            s, r = s.at[k], r.at[k]
        return pltpu.make_async_remote_copy(
            src_ref=src, dst_ref=dst, send_sem=s, recv_sem=r, device_id=to, device_id_type=MESH
        )

    barrier = pltpu.get_barrier_semaphore()

    def greet(to):
        pl.semaphore_signal(barrier, inc=1, device_id=to, device_id_type=MESH)

    for to in (sib, xright, xleft):
        greet(to)
    pl.when(has_left)(lambda: greet(zleft))
    pl.when(has_right)(lambda: greet(zright))
    pl.when(feeds)(lambda: greet(before))
    pl.when(fed)(lambda: greet(after))
    partners = 3 + has_left.astype(jnp.int32) + has_right.astype(jnp.int32)
    partners = partners + feeds.astype(jnp.int32) + fed.astype(jnp.int32)
    far = [mid + 2 * p for p in range(spread)]
    near = [2 * p for p in range(spread)]
    for p in range(spread):
        pl.when(cross)(lambda: greet(at_time(near[p])))
        pl.when(tm == near[p])(lambda: greet(at_time(far[p] if p else mid)))
        if p:
            pl.when(tm == far[p])(lambda: greet(at_time(mid)))

    relaying = jnp.logical_and(is0, jnp.logical_not(crossed))
    partners = partners + jnp.where(crossed, spread, relaying.astype(jnp.int32))

    pts = pts_ref[...]
    norm = to_row(jnp.sum(pts * pts, axis=1, keepdims=True)) * (scale / feats)
    trow = tpot_ref[...] * scale - norm
    srow = spot_ref[...] * scale - norm - math.log2(population)

    def put(buf, b):
        for i in range(2):
            buf[b, i * hrow : i * hrow + half, :] = pts[i * half : (i + 1) * half]
            pair = jnp.concatenate(
                [trow[:, i * half : (i + 1) * half], srow[:, i * half : (i + 1) * half], jnp.zeros((6, half), F32)], axis=0
            )
            buf[b, i * hrow + half : (i + 1) * hrow, :] = jnp.concatenate(
                [pair, jnp.zeros((8, feats - half), F32)], axis=1
            )

    pl.when(is0)(lambda: put(mbuf, x))
    pl.when(is1)(lambda: put(sbuf, z))

    pl.semaphore_wait(barrier, partners)

    mine = pl.ds(pl.multiple_of(core * hrow, 8), hrow)
    other = pl.ds(pl.multiple_of((1 - core) * hrow, 8), hrow)
    mine_rows = pl.ds(pl.multiple_of(core * half, 8), half)
    other_rows = pl.ds(pl.multiple_of((1 - core) * half, 8), half)

    def chunk(c):
        size = piece + (8 if c == CH - 1 else 0)
        return pl.ds(pl.multiple_of(core * hrow + c * piece, 8), size)

    def own_copy(i):
        ref = sbuf.at[z, pl.ds(i * hrow, hrow)]
        return rdma(ref, ref, "own", sib, i)

    def tm_copy():
        return rdma(mbuf.at[x], mbuf.at[x], "tm", before)

    h0, h1 = pl.ds(0, hrow), pl.ds(hrow, hrow)

    def mx_send(k):
        if k < 2:
            ref = mbuf.at[x]
        else:
            ref = mbuf.at[x3, h0] if k == 2 else mbuf.at[x1, h1]
        return rdma(ref, ref, "mx", xright if k % 2 == 0 else xleft, k)

    def mx_arrival(k):
        if k < 2:
            ref = mbuf.at[x3] if k == 0 else mbuf.at[x1]
        else:
            ref = mbuf.at[x2, h0] if k == 2 else mbuf.at[x2, h1]
        return rdma(ref, ref, "mx", xright, k)

    pieces = []
    for i in range(2):
        at = i * hrow
        pieces += [(at, half // 2), (at + half // 2, half // 2 + 8)]

    def fx_first(p):
        at, size = pieces[p]
        dst = v["relay"].at[pl.ds(0, size)]
        return rdma(mbuf.at[x, pl.ds(at, size)], dst, "fx", at_time(far[p] if p else near[p]), p)

    def fx_second(p):
        ref = v["relay"].at[pl.ds(0, pieces[p][1])]
        return rdma(ref, ref, "fx", at_time(near[p]), p)

    def fx_third(p):
        at, size = pieces[p]
        src = v["relay"].at[pl.ds(0, size)]
        return rdma(src, mbuf.at[x, pl.ds(at, size)], "fx", at_time(mid - 1), p)

    quarter = rows // spread

    def bx_first(p):
        return rdma(gm.at[x, pl.ds(p * quarter, quarter)], v["back"], "bx", at_time(near[p]), p)

    def bx_second(p):
        dst = v["back"] if p else v["gtm_in"].at[pl.ds(0, quarter)]
        return rdma(v["back"], dst, "bx", at_time(far[p] if p else mid), p)

    def bx_third(p):
        return rdma(v["back"], v["gtm_in"].at[pl.ds(p * quarter, quarter)], "bx", at_time(mid), p)

    @pl.when(is1)
    def _():
        own_copy(0).start()
        own_copy(1).start()

    @pl.when(is0)
    def _():
        pl.when(feeds)(lambda: tm_copy().start())

        @pl.when(crossed)
        def _():
            for p in range(spread):
                fx_first(p).start()

        mx_send(0).start()
        mx_send(1).start()
        own_copy(0).wait_recv()

    def zr_copy(s, c, b):
        ref = sbuf.at[b, chunk(c)]
        return rdma(ref, ref, "zr", zright, s * CH + c)

    def zl_copy(s, c, b):
        ref = sbuf.at[b, chunk(c)]
        return rdma(ref, ref, "zl", zleft, s * CH + c)

    def sib_copy(b, window):
        ref = sbuf.at[b, window]
        return rdma(ref, ref, "sib", sib, b)

    wait_m = jnp.where(cross, nz, 2)
    mx_step = jnp.where(cross, nz + 1, jnp.where(is0, 2, 4))
    first = jnp.where(cross, nz + 2, jnp.where(is0, 4, 6))
    late = jnp.logical_or(cross, tm == mid - 2)
    chain_at = jnp.where(late, nz + 3, nz + 1)
    ahead = jnp.maximum(nz - first, 0)

    def order(n):
        k = lax.rem(n + nz - ahead, nz)
        low = jnp.minimum(z, last - z)
        single = last - 2 * low
        d = (k - single) // 2
        b = jnp.where(k < single, last - k, jnp.where(lax.rem(k - single, 2) == 0, 2 * low - d, d))
        return jnp.where(z < nz - nz // 2, b, last - b)

    def pe_copy(b, window):
        return rdma(part.at[b, window], v["sib_part"].at[b], "pe", sib, b)

    def prepare():
        mx_arrival(2).wait_recv()
        mx_arrival(3).wait_recv()
        for j in range(nx):
            for i in range(2):
                at = j * rows + i * half
                hi, lo = split(mbuf[j, i * hrow : i * hrow + half, :])
                mhi[at : at + half, :] = hi
                mlo[at : at + half, :] = lo
                pair = mbuf[j, i * hrow + half : (i + 1) * hrow, 0:half]
                brow[0:1, at : at + half] = jnp.where(is0, pair[1:2], pair[0:1])

    def tile_open(b):
        for i in range(2):
            at = slice(i * half, (i + 1) * half)
            s = sbuf[b, i * hrow : i * hrow + half, :]
            hi, lo = split(s)
            v["shi"][at, :] = hi
            v["slo"][at, :] = lo
            hi, lo = split(s.T)
            v["thi"][:, at] = hi
            v["tlo"][:, at] = lo
            pair = sbuf[b, i * hrow + half : (i + 1) * hrow, 0:half]
            v["acol"][at, :] = jnp.broadcast_to(to_col(jnp.where(is0, pair[0:1], pair[1:2])), (half, half))

    def tile_part(b, c):
        width = nx * rows // CH
        at = slice(c * width, (c + 1) * width)
        m = (mhi[at, :], mlo[at, :])
        g = dot3((v["shi"][...], v["slo"][...]), m, ((1,), (1,)))
        w = jnp.exp2(g * (2.0 * scale / feats) + v["acol"][:, 0:1] + brow[0:1, at])
        total = jnp.sum(w, axis=1, keepdims=True)
        csum[0:1, at] += jnp.sum(w, axis=0, keepdims=True)
        ww = split(w)
        moved = dot3(ww, m, ((1,), (0,)))
        gmt[:, at] += dot3((v["thi"][...], v["tlo"][...]), ww, ((1,), (0,)))
        for i in range(2):
            r = slice(i * half, (i + 1) * half)
            term = total[r] * sbuf[b, i * hrow : i * hrow + half, :] - moved[r]
            part[b, r, :] = term if c == 0 else part[b, r, :] + term

    gmt[...] = jnp.zeros_like(gmt)
    csum[...] = jnp.zeros_like(csum)

    g0, g1 = pl.ds(0, half), pl.ds(half, half)

    def gx_copy(k):
        src, dst = [
            (gm.at[x2, g0], v["gmid"].at[0]),
            (gm.at[x2, g1], v["gmid"].at[1]),
            (gm.at[x1, g1], gx_in.at[0, g1]),
            (gm.at[x3, g0], gx_in.at[1, g0]),
            (gm.at[x1, g0], gx_in.at[0, g0]),
            (gm.at[x3, g1], gx_in.at[1, g1]),
        ][k]
        return rdma(src, dst, "gx", xright if k % 2 == 0 else xleft, k)

    def finish_m(j):
        at = pl.ds(pl.multiple_of(j * rows, rows), rows)
        ccol = to_col(csum[0:1, at])
        g = gmt[:, at].T
        for i in range(2):
            lo = i * half
            gm[j, lo : lo + half, :] = ccol[lo : lo + half] * mbuf[j, i * hrow : i * hrow + half, :] - g[lo : lo + half]

    def gt_copy():
        return rdma(gm.at[x], v["gtm_in"], "gt", after)

    def cr_copy(b, c):
        ref = v["rsum"].at[b, pl.ds(c * piece, piece)]
        return rdma(ref, ref, "cr", zright, b * CH + c)

    def cl_copy(b, c):
        ref = v["lsum"].at[b, pl.ds(c * piece, piece)]
        return rdma(ref, ref, "cl", zleft, b * CH + c)

    def link(b, c, copy, total, begun):
        r = pl.ds(c * piece, piece)
        mine_r = pl.ds(pl.multiple_of(core * half + c * piece, 8), piece)

        @pl.when(begun)
        def _():
            copy(b, c).wait_recv()
            total[b, r, :] = total[b, r, :] + part[b, mine_r, :] + v["sib_part"][b, r, :]

        @pl.when(jnp.logical_not(begun))
        def _():
            total[b, r, :] = part[b, mine_r, :] + v["sib_part"][b, r, :]

        copy(b, c).start()

    def step(s, carry):
        n = s - first
        has_tile = jnp.logical_and(n >= 0, n < nz)
        b = order(jnp.clip(n, 0, last))
        computes = jnp.logical_and(has_tile, active)
        relays = jnp.logical_and(s >= 1, s <= last)
        from_left = jnp.logical_and(relays, z - s >= 0)
        from_right = jnp.logical_and(relays, z + s <= last)

        for p in range(1, spread):

            @pl.when(jnp.logical_and(s == 1, tm == far[p]))
            def _():
                fx_second(p).wait_recv()
                fx_second(p).start()

        for p in range(spread):

            @pl.when(jnp.logical_and(s == nz - 2, tm == near[p]))
            def _():
                fx_second(p).wait_recv()
                fx_third(p).start()

        @pl.when(s == wait_m)
        def _():
            @pl.when(fed)
            def _():
                tm_copy().wait_recv()

            @pl.when(cross)
            def _():
                for p in range(spread):
                    at, size = pieces[p]
                    ref = mbuf.at[x, pl.ds(at, size)]
                    rdma(ref, ref, "fx", at_time(mid - 1), p).wait_recv()

            @pl.when(jnp.logical_or(fed, cross))
            def _():
                mx_send(0).start()
                mx_send(1).start()

        @pl.when(jnp.logical_and(active, s == mx_step))
        def _():
            mx_arrival(0).wait_recv()
            mx_send(2).start()
            mx_arrival(1).wait_recv()
            mx_send(3).start()

        pl.when(jnp.logical_and(active, s == first))(prepare)

        @pl.when(has_tile)
        def _():
            @pl.when(b != z)
            def _():
                sib_copy(b, other).wait_recv()

            @pl.when(jnp.logical_and(b == z, is0))
            def _():
                own_copy(1).wait_recv()

        for c in range(CH):

            @pl.when(s == 0)
            def _():
                pl.when(has_right)(lambda: zr_copy(0, c, z).start())
                pl.when(has_left)(lambda: zl_copy(0, c, z).start())

            @pl.when(from_left)
            def _():
                zr_copy(s - 1, c, z - s).wait_recv()

                @pl.when(jnp.logical_and(has_right, s < last))
                def _():
                    zr_copy(s, c, z - s).start()

                if c == CH - 1:
                    sib_copy(z - s, mine).start()

            @pl.when(from_right)
            def _():
                zl_copy(s - 1, c, z + s).wait_recv()

                @pl.when(jnp.logical_and(has_left, s < last))
                def _():
                    zl_copy(s, c, z + s).start()

                if c == CH - 1:
                    sib_copy(z + s, mine).start()

            @pl.when(computes)
            def _():
                if c == 0:
                    tile_open(b)
                tile_part(b, c)

        @pl.when(has_tile)
        def _():
            @pl.when(jnp.logical_not(active))
            def _():
                part[b] = jnp.zeros((rows, feats), F32)

            pe_copy(b, other_rows).start()

        cs = s - chain_at
        linked = jnp.logical_and(cs >= 0, cs < last)
        goes_right = jnp.logical_and(linked, jnp.logical_and(has_right, cs >= z))
        goes_left = jnp.logical_and(linked, jnp.logical_and(has_left, cs >= last - z))
        br, bl = last - cs + z, cs + z - last
        pl.when(goes_right)(lambda: pe_copy(br, mine_rows).wait_recv())
        pl.when(goes_left)(lambda: pe_copy(bl, mine_rows).wait_recv())
        for c in range(CH):
            pl.when(goes_right)(lambda: link(br, c, cr_copy, v["rsum"], has_left))
            pl.when(goes_left)(lambda: link(bl, c, cl_copy, v["lsum"], has_right))

        done = s - first - nz

        @pl.when(jnp.logical_and(active, done == 0))
        def _():
            finish_m(x2)
            gx_copy(0).start()
            gx_copy(1).start()
            finish_m(x1)
            gx_copy(2).start()
            finish_m(x3)
            gx_copy(3).start()
            finish_m(x)

        @pl.when(jnp.logical_and(active, done == 2))
        def _():
            gx_copy(0).wait_recv()
            gm[x1, g0, :] = gm[x1, g0, :] + v["gmid"][0]
            gx_copy(4).start()
            gx_copy(1).wait_recv()
            gm[x3, g1, :] = gm[x3, g1, :] + v["gmid"][1]
            gx_copy(5).start()

        @pl.when(jnp.logical_and(active, done == 4))
        def _():
            for k in range(2, 6):
                gx_copy(k).wait_recv()
            gm[x] = gm[x] + gx_in[0] + gx_in[1]
            pl.when(fed)(lambda: gt_copy().start())

            @pl.when(cross)
            def _():
                for p in range(spread):
                    bx_first(p).start()

        return carry

    lax.fori_loop(0, 2 * nz + 7, step, 0)

    pe_copy(z, mine_rows).wait_recv()
    fin[0] = part[z, mine_rows, :] + v["sib_part"][z]
    for c in range(CH):
        r = pl.ds(c * piece, piece)

        @pl.when(has_left)
        def _():
            cr_copy(z, c).wait_recv()
            fin[0, r, :] = fin[0, r, :] + v["rsum"][z, r, :]

        @pl.when(has_right)
        def _():
            cl_copy(z, c).wait_recv()
            fin[0, r, :] = fin[0, r, :] + v["lsum"][z, r, :]

    fin_copy = rdma(fin.at[0], fin.at[1], "fi", sib)

    @pl.when(is0)
    def _():
        fin_copy.start()
        out_ref[...] = gm[x]

        @pl.when(feeds)
        def _():
            gt_copy().wait_recv()
            out_ref[...] = out_ref[...] + v["gtm_in"][...]

    for p in range(spread):

        @pl.when(tm == near[p])
        def _():
            bx_second(p).wait_recv() if p else bx_first(p).wait_recv()
            bx_second(p).start()

    for p in range(1, spread):

        @pl.when(tm == far[p])
        def _():
            bx_second(p).wait_recv()
            bx_third(p).start()

    @pl.when(crossed)
    def _():
        for p in range(spread):
            bx_third(p).wait_recv()
        out_ref[...] = out_ref[...] + v["gtm_in"][...]

    @pl.when(is1)
    def _():
        out_ref[half:, :] = fin[0]
        fin_copy.wait_recv()
        out_ref[0:half, :] = fin[1]

    @pl.when(is1)
    def _():
        own_copy(0).wait_send()
        own_copy(1).wait_send()

    pl.when(is0)(lambda: fin_copy.wait_send())
    pl.when(feeds)(lambda: tm_copy().wait_send())
    pl.when(fed)(lambda: gt_copy().wait_send())
    for p in range(spread):

        @pl.when(crossed)
        def _():
            fx_first(p).wait_send()

        @pl.when(cross)
        def _():
            bx_first(p).wait_send()

        @pl.when(tm == near[p])
        def _():
            fx_third(p).wait_send()
            bx_second(p).wait_send()

        if p:

            @pl.when(tm == far[p])
            def _():
                fx_second(p).wait_send()
                bx_third(p).wait_send()

    @pl.when(active)
    def _():
        for k in range(4):
            mx_send(k).wait_send()
        for k in range(6):
            gx_copy(k).wait_send()

    def drain(b, carry):
        pe_copy(b, other_rows).wait_send()

        @pl.when(b != z)
        def _():
            sib_copy(b, mine).wait_send()

        for c in range(CH):
            pl.when(jnp.logical_and(has_right, b <= z))(lambda: zr_copy(z - b, c, b).wait_send())
            pl.when(jnp.logical_and(has_left, b >= z))(lambda: zl_copy(b - z, c, b).wait_send())
            pl.when(jnp.logical_and(has_right, b > z))(lambda: cr_copy(b, c).wait_send())
            pl.when(jnp.logical_and(has_left, b < z))(lambda: cl_copy(b, c).wait_send())
        return carry

    lax.fori_loop(0, nz, drain, 0)


def local(dims, particles, source_pots, target_pots):
    times, nx, nz, rows, feats = dims
    half = rows // 2
    spread = times // 4
    dma = pltpu.SemaphoreType.DMA
    shapes = [
        ((nz, rows + 16, feats), F32),
        ((nx, rows + 16, feats), F32),
        ((nx * rows, feats), BF16),
        ((nx * rows, feats), BF16),
        ((8, nx * rows), F32),
        ((nz, rows, feats), F32),
        ((nz, half, feats), F32),
        ((nz, half, feats), F32),
        ((nz, half, feats), F32),
        ((feats, nx * rows), F32),
        ((8, nx * rows), F32),
        ((nx, rows, feats), F32),
        ((2, rows, feats), F32),
        ((2, half, feats), F32),
        ((rows, feats), F32),
        ((2, half, feats), F32),
        ((half // 2 + 8, feats), F32),
        ((rows // spread, feats), F32),
        ((rows, feats), BF16),
        ((rows, feats), BF16),
        ((feats, rows), BF16),
        ((feats, rows), BF16),
        ((rows, half), F32),
    ]
    scratch = [pltpu.VMEM(shape, kind) for shape, kind in shapes]
    line = nz * CH
    for count in (2, line, line, nz, 0, 4, nz, line, line, 6, 0, 0, spread, spread):
        kind = dma((count,)) if count else dma
        scratch += [kind, kind]
    out = pl.pallas_call(
        functools.partial(kernel, dims),
        out_shape=jax.ShapeDtypeStruct((rows, feats), F32),
        in_specs=[pl.BlockSpec(memory_space=pltpu.VMEM)] * 3,
        out_specs=pl.BlockSpec(memory_space=pltpu.VMEM),
        scratch_shapes=scratch,
        compiler_params=pltpu.CompilerParams(
            collective_id=0, has_side_effects=True, vmem_limit_bytes=56 * 2**20
        ),
    )(particles[0], source_pots, target_pots)
    return out[None]


def solution(mesh):
    times, nx, nz = mesh.shape["tm"], mesh.shape["row"], mesh.shape["col"]

    def program(particles, source_pots, target_pots):
        rows = particles.shape[1] // (nx * nz)
        dims = (times, nx, nz, rows, particles.shape[2])
        return jax.shard_map(
            functools.partial(local, dims),
            mesh=mesh,
            in_specs=(P("tm", ("row", "col"), None), P("tm", ("row", "col")), P("tm", ("row", "col"))),
            out_specs=P("tm", ("row", "col"), None),
            check_vma=False,
        )(particles, source_pots, target_pots)

    return program
```

```python
import functools
import math

import jax
import jax.numpy as jnp
from jax import lax
from jax.experimental import pallas as pl
from jax.experimental.pallas import tpu as pltpu
from jax.sharding import PartitionSpec as P

EPS = 0.1
MESH = pl.DeviceIdType.MESH
F32 = jnp.float32
BF16 = jnp.bfloat16


def split(x):
    hi = x.astype(BF16)
    return hi, (x - hi.astype(F32)).astype(BF16)


def dot(a, b, dims):
    return lax.dot_general(a, b, (dims, ((), ())), preferred_element_type=F32)


def dot3(a, b, dims):
    return dot(a[0], b[0], dims) + dot(a[0], b[1], dims) + dot(a[1], b[0], dims)


def eye(n):
    return lax.broadcasted_iota(jnp.int32, (n, n), 0) == lax.broadcasted_iota(jnp.int32, (n, n), 1)


def to_row(col):
    n = col.shape[0]
    return jnp.sum(jnp.where(eye(n), col, 0.0), axis=0, keepdims=True)


def to_col(row):
    n = row.shape[1]
    return jnp.sum(jnp.where(eye(n), row, 0.0), axis=1, keepdims=True)


BUFS = (
    "sbuf", "mbuf", "mhi", "mlo", "brow", "part", "sib_part", "rsum", "gmt", "csum", "gm",
    "gx_in", "gmid", "gtm_in", "fin", "relay", "back", "shi", "slo", "thi", "tlo", "acol",
)
SEMS = (
    "own", "zr", "sib", "tm", "mx", "pe", "cr", "gx", "gt", "fi",
    "fx", "bx",
)
CH = 4


def kernel(dims, pts_ref, spot_ref, tpot_ref, out_ref, *scratch):
    times, nx, nz, rows, feats = dims
    half = rows // 2
    hrow = half + 8
    piece = rows // CH
    last = nz - 1
    run = nz // 2
    mid = times // 2
    spread = mid // 2
    population = rows * nx * nz
    scale = math.log2(math.e) / EPS
    v = dict(zip(BUFS, scratch))
    sems = {name: scratch[len(BUFS) + 2 * i : len(BUFS) + 2 * i + 2] for i, name in enumerate(SEMS)}
    sbuf, mbuf, part, gm, fin = v["sbuf"], v["mbuf"], v["part"], v["gm"], v["fin"]
    mhi, mlo, brow, gmt, csum = v["mhi"], v["mlo"], v["brow"], v["gmt"], v["csum"]
    gx_in = v["gx_in"]

    tm, x, z = lax.axis_index("tm"), lax.axis_index("row"), lax.axis_index("col")
    core = lax.rem(tm, 2)
    is0, is1 = core == 0, core == 1
    active = tm < times - 1
    cross = tm == mid - 1
    crossed = tm == mid
    fed = jnp.logical_and(jnp.logical_and(is1, active), jnp.logical_not(cross))
    feeds = jnp.logical_and(jnp.logical_and(is0, tm > 0), jnp.logical_not(crossed))
    place = jnp.where(is0, z, last - z)
    has_prev, has_next = place > 0, place < last
    way = 1 - 2 * core
    forth = (tm, x, jnp.clip(z + way, 0, last))
    back_to = (tm, x, jnp.clip(z - way, 0, last))
    sib = (tm + 1 - 2 * core, x, z)
    before, after = (jnp.maximum(tm - 1, 0), x, z), (jnp.minimum(tm + 1, times - 1), x, z)
    x1, x2, x3 = lax.rem(x + 1, nx), lax.rem(x + 2, nx), lax.rem(x + 3, nx)
    xright, xleft = (tm, x1, z), (tm, x3, z)

    def at_time(t):
        return (t, x, z)

    def rdma(src, dst, name, to, k=None):
        s, r = sems[name]
        if k is not None:
            s, r = s.at[k], r.at[k]
        return pltpu.make_async_remote_copy(
            src_ref=src, dst_ref=dst, send_sem=s, recv_sem=r, device_id=to, device_id_type=MESH
        )

    barrier = pltpu.get_barrier_semaphore()

    def greet(to):
        pl.semaphore_signal(barrier, inc=1, device_id=to, device_id_type=MESH)

    for to in (sib, xright, xleft):
        greet(to)
    pl.when(has_prev)(lambda: greet(back_to))
    pl.when(feeds)(lambda: greet(before))
    pl.when(fed)(lambda: greet(after))
    partners = 3 + has_next.astype(jnp.int32)
    partners = partners + feeds.astype(jnp.int32) + fed.astype(jnp.int32)
    far = [mid + 2 * p for p in range(spread)]
    near = [2 * p for p in range(spread)]
    for p in range(spread):
        pl.when(cross)(lambda: greet(at_time(near[p])))
        pl.when(tm == near[p])(lambda: greet(at_time(far[p] if p else mid)))
        if p:
            pl.when(tm == far[p])(lambda: greet(at_time(mid)))

    relaying = jnp.logical_and(is0, jnp.logical_not(crossed))
    partners = partners + jnp.where(crossed, spread, relaying.astype(jnp.int32))

    pts = pts_ref[...]
    norm = to_row(jnp.sum(pts * pts, axis=1, keepdims=True)) * (scale / feats)
    trow = tpot_ref[...] * scale - norm
    srow = spot_ref[...] * scale - norm - math.log2(population)

    def put(buf, b):
        for i in range(2):
            buf[b, i * hrow : i * hrow + half, :] = pts[i * half : (i + 1) * half]
            pair = jnp.concatenate(
                [trow[:, i * half : (i + 1) * half], srow[:, i * half : (i + 1) * half], jnp.zeros((6, half), F32)], axis=0
            )
            buf[b, i * hrow + half : (i + 1) * hrow, :] = jnp.concatenate(
                [pair, jnp.zeros((8, feats - half), F32)], axis=1
            )

    pl.when(is0)(lambda: put(mbuf, x))
    pl.when(is1)(lambda: put(sbuf, z))

    pl.semaphore_wait(barrier, partners)

    def chunk(g, k):
        return pl.ds(pl.multiple_of(g * hrow + k * (half // 2), 8), half // 2 + 8 * k)

    def blk(i):
        return jnp.where(is0, i, last - i)

    def own_copy(i):
        ref = sbuf.at[z, pl.ds(i * hrow, hrow)]
        return rdma(ref, ref, "own", sib, i)

    def tm_copy():
        return rdma(mbuf.at[x], mbuf.at[x], "tm", before)

    h0, h1 = pl.ds(0, hrow), pl.ds(hrow, hrow)

    def mx_send(k):
        if k < 2:
            ref = mbuf.at[x]
        else:
            ref = mbuf.at[x3, h0] if k == 2 else mbuf.at[x1, h1]
        return rdma(ref, ref, "mx", xright if k % 2 == 0 else xleft, k)

    def mx_arrival(k):
        if k < 2:
            ref = mbuf.at[x3] if k == 0 else mbuf.at[x1]
        else:
            ref = mbuf.at[x2, h0] if k == 2 else mbuf.at[x2, h1]
        return rdma(ref, ref, "mx", xright, k)

    pieces = []
    for i in range(2):
        at = i * hrow
        pieces += [(at, half // 2), (at + half // 2, half // 2 + 8)]

    def fx_first(p):
        at, size = pieces[p]
        dst = v["relay"].at[pl.ds(0, size)]
        return rdma(mbuf.at[x, pl.ds(at, size)], dst, "fx", at_time(far[p] if p else near[p]), p)

    def fx_second(p):
        ref = v["relay"].at[pl.ds(0, pieces[p][1])]
        return rdma(ref, ref, "fx", at_time(near[p]), p)

    def fx_third(p):
        at, size = pieces[p]
        src = v["relay"].at[pl.ds(0, size)]
        return rdma(src, mbuf.at[x, pl.ds(at, size)], "fx", at_time(mid - 1), p)

    quarter = rows // spread

    def bx_first(p):
        return rdma(gm.at[x, pl.ds(p * quarter, quarter)], v["back"], "bx", at_time(near[p]), p)

    def bx_second(p):
        dst = v["back"] if p else v["gtm_in"].at[pl.ds(0, quarter)]
        return rdma(v["back"], dst, "bx", at_time(far[p] if p else mid), p)

    def bx_third(p):
        return rdma(v["back"], v["gtm_in"].at[pl.ds(p * quarter, quarter)], "bx", at_time(mid), p)

    def zr_part(s, g, k, b):
        ref = sbuf.at[b, chunk(g, k)]
        return rdma(ref, ref, "zr", forth, s * CH + 2 * g + k)

    def zr_copy(s, c, b):
        return zr_part(s, c // 2, c % 2, b)

    def sib_copy(b):
        return rdma(sbuf.at[b], sbuf.at[b], "sib", sib, b)

    @pl.when(is1)
    def _():
        own_copy(0).start()
        own_copy(1).start()
        for c in range(CH):
            pl.when(has_next)(lambda: zr_copy(0, c, z).start())

    @pl.when(is0)
    def _():
        pl.when(feeds)(lambda: tm_copy().start())

        @pl.when(crossed)
        def _():
            for p in range(spread):
                fx_first(p).start()

        mx_send(0).start()
        mx_send(1).start()
        for i in range(2):
            own_copy(i).wait_recv()
            for c in (2 * i, 2 * i + 1):
                pl.when(has_next)(lambda: zr_copy(0, c, z).start())

    chain_at = nz + 1
    near_at, far_at = run, 1
    wait_m = jnp.where(cross, run + 1, 1)
    mx_step = jnp.where(cross, run + 2, jnp.where(is0, 1, 3))
    first = jnp.where(cross, nz, jnp.where(is0, 3, 4))
    pace = jnp.where(cross, 2, 1)
    ahead = nz - first

    def order(n):
        k = jnp.where(n < ahead, last - n, n - ahead)
        low = jnp.minimum(z, last - z)
        single = last - 2 * low
        d = (k - single) // 2
        b = jnp.where(k < single, last - k, jnp.where(lax.rem(k - single, 2) == 0, 2 * low - d, d))
        return jnp.where(z < nz - nz // 2, b, last - b)

    def pe_copy(b):
        return rdma(part.at[b], v["sib_part"].at[b], "pe", sib, b)

    def prepare():
        mx_arrival(2).wait_recv()
        mx_arrival(3).wait_recv()
        for j in range(nx):
            for i in range(2):
                at = j * rows + i * half
                hi, lo = split(mbuf[j, i * hrow : i * hrow + half, :])
                mhi[at : at + half, :] = hi
                mlo[at : at + half, :] = lo
                pair = mbuf[j, i * hrow + half : (i + 1) * hrow, 0:half]
                brow[0:1, at : at + half] = jnp.where(is0, pair[1:2], pair[0:1])

    def tile_open(b):
        for i in range(2):
            at = slice(i * half, (i + 1) * half)
            s = sbuf[b, i * hrow : i * hrow + half, :]
            hi, lo = split(s)
            v["shi"][at, :] = hi
            v["slo"][at, :] = lo
            hi, lo = split(s.T)
            v["thi"][:, at] = hi
            v["tlo"][:, at] = lo
            pair = sbuf[b, i * hrow + half : (i + 1) * hrow, 0:half]
            v["acol"][at, :] = jnp.broadcast_to(to_col(jnp.where(is0, pair[0:1], pair[1:2])), (half, half))

    def tile_part(b, c):
        width = nx * rows // 2
        at = pl.ds(pl.multiple_of(c * width, width), width)
        m = (mhi[at, :], mlo[at, :])
        g = dot3((v["shi"][...], v["slo"][...]), m, ((1,), (1,)))
        w = jnp.exp2(g * (2.0 * scale / feats) + v["acol"][:, 0:1] + brow[0:1, at])
        total = jnp.sum(w, axis=1, keepdims=True)
        csum[0:1, at] += jnp.sum(w, axis=0, keepdims=True)
        ww = split(w)
        moved = dot3(ww, m, ((1,), (0,)))
        gmt[:, at] += dot3((v["thi"][...], v["tlo"][...]), ww, ((1,), (0,)))
        for i in range(2):
            r = slice(i * half, (i + 1) * half)
            part[b, r, :] = part[b, r, :] + (total[r] * sbuf[b, i * hrow : i * hrow + half, :] - moved[r])

    gmt[...] = jnp.zeros_like(gmt)
    csum[...] = jnp.zeros_like(csum)

    g0, g1 = pl.ds(0, half), pl.ds(half, half)

    def gx_copy(k):
        src, dst = [
            (gm.at[x2, g0], v["gmid"].at[0]),
            (gm.at[x2, g1], v["gmid"].at[1]),
            (gm.at[x1, g1], gx_in.at[0, g1]),
            (gm.at[x3, g0], gx_in.at[1, g0]),
            (gm.at[x1, g0], gx_in.at[0, g0]),
            (gm.at[x3, g1], gx_in.at[1, g1]),
        ][k]
        return rdma(src, dst, "gx", xright if k % 2 == 0 else xleft, k)

    def finish_m(j):
        at = pl.ds(pl.multiple_of(j * rows, rows), rows)
        ccol = to_col(csum[0:1, at])
        g = gmt[:, at].T
        for i in range(2):
            lo = i * half
            gm[j, lo : lo + half, :] = ccol[lo : lo + half] * mbuf[j, i * hrow : i * hrow + half, :] - g[lo : lo + half]

    def gt_copy():
        return rdma(gm.at[x], v["gtm_in"], "gt", after)

    def cr_copy(b, c):
        ref = v["rsum"].at[b, pl.ds(c * piece, piece)]
        return rdma(ref, ref, "cr", forth, b * CH + c)

    def fi_copy(c):
        r = pl.ds(c * piece, piece)
        return rdma(v["rsum"].at[z, r], fin.at[r], "fi", sib, c)

    def step(s, carry):
        @pl.when(jnp.logical_and(is0, jnp.logical_or(s == far_at, s == near_at)))
        def _():
            for p in range(1, spread):

                @pl.when(jnp.logical_and(s == far_at, tm == far[p]))
                def _():
                    fx_second(p).wait_recv()
                    fx_second(p).start()

            for p in range(spread):

                @pl.when(jnp.logical_and(s == near_at, tm == near[p]))
                def _():
                    fx_second(p).wait_recv()
                    fx_third(p).start()

        @pl.when(s <= first)
        def _():
            @pl.when(s == wait_m)
            def _():
                @pl.when(fed)
                def _():
                    tm_copy().wait_recv()

                @pl.when(cross)
                def _():
                    for p in range(spread):
                        at, size = pieces[p]
                        ref = mbuf.at[x, pl.ds(at, size)]
                        rdma(ref, ref, "fx", at_time(mid - 1), p).wait_recv()

                @pl.when(jnp.logical_or(fed, cross))
                def _():
                    mx_send(0).start()
                    mx_send(1).start()

            @pl.when(jnp.logical_and(active, s == mx_step))
            def _():
                mx_arrival(0).wait_recv()
                mx_send(2).start()
                mx_arrival(1).wait_recv()
                mx_send(3).start()

            pl.when(jnp.logical_and(active, s == first))(prepare)

        relays = jnp.logical_and(s <= last, s <= place)
        onward = jnp.logical_and(relays, jnp.logical_and(has_next, s < last))
        at = blk(place - s)

        def unit(u, carry):
            c = lax.rem(u, 2)
            n = (s - first) * pace + u // 2
            b = order(jnp.clip(n, 0, last))
            has_tile = jnp.logical_and(n >= 0, n < nz)

            @pl.when(jnp.logical_and(relays, u < 2))
            def _():
                for k in range(2):
                    zr_part(s - 1, u, k, at).wait_recv()
                    pl.when(onward)(lambda: zr_part(s, u, k, at).start())

            @pl.when(has_tile)
            def _():
                @pl.when(c == 0)
                def _():
                    pl.when(jnp.where(is0, b > z, b < z))(lambda: sib_copy(b).wait_recv())
                    part[b] = jnp.zeros((rows, feats), F32)
                    pl.when(active)(lambda: tile_open(b))

                pl.when(active)(lambda: tile_part(b, c))

                @pl.when(jnp.logical_and(c == 1, jnp.where(is0, b <= z, b > z)))
                def _():
                    pe_copy(b).start()

            return carry

        units = jnp.where(jnp.logical_or(s <= last, s < first + nz // pace), 2 * jnp.where(s < first, 1, pace), 0)
        lax.fori_loop(0, units, unit, 0)
        pl.when(relays)(lambda: sib_copy(at).start())

        cs = s - chain_at

        @pl.when(jnp.logical_and(jnp.logical_and(cs >= place, cs < last), has_next))
        def _():
            t = blk(last - cs + place)
            pe_copy(t).wait_recv()
            for c in range(CH):
                r = pl.ds(c * piece, piece)

                @pl.when(has_prev)
                def _():
                    cr_copy(t, c).wait_recv()
                    v["rsum"][t, r, :] = v["rsum"][t, r, :] + (part[t, r, :] + v["sib_part"][t, r, :])

                @pl.when(jnp.logical_not(has_prev))
                def _():
                    v["rsum"][t, r, :] = part[t, r, :] + v["sib_part"][t, r, :]

                cr_copy(t, c).start()

        done = s - first - nz // pace

        @pl.when(jnp.logical_and(active, done >= 0))
        def _():
            @pl.when(done == 0)
            def _():
                finish_m(x2)
                gx_copy(0).start()
                gx_copy(1).start()
                finish_m(x1)
                gx_copy(2).start()
                finish_m(x3)
                gx_copy(3).start()
                finish_m(x)

            @pl.when(done == 1)
            def _():
                gx_copy(0).wait_recv()
                gm[x1, g0, :] = gm[x1, g0, :] + v["gmid"][0]
                gx_copy(4).start()
                gx_copy(1).wait_recv()
                gm[x3, g1, :] = gm[x3, g1, :] + v["gmid"][1]
                gx_copy(5).start()

            @pl.when(done == 2)
            def _():
                for k in range(2, 6):
                    gx_copy(k).wait_recv()
                gm[x] = gm[x] + gx_in[0] + gx_in[1]
                pl.when(fed)(lambda: gt_copy().start())

                @pl.when(cross)
                def _():
                    for p in range(spread):
                        bx_first(p).start()

        return carry

    steps = jnp.maximum(first + nz // pace + 3, chain_at + last)
    lax.fori_loop(1, steps, step, 0)

    @pl.when(is0)
    def _():
        @pl.when(has_prev)
        def _():
            for c in range(CH):
                cr_copy(z, c).wait_recv()
                fi_copy(c).start()

        for p in range(spread):

            @pl.when(tm == near[p])
            def _():
                bx_first(p).wait_recv()
                bx_second(p).start()

        out_ref[...] = gm[x]

        @pl.when(feeds)
        def _():
            gt_copy().wait_recv()
            out_ref[...] = out_ref[...] + v["gtm_in"][...]

    for p in range(1, spread):

        @pl.when(tm == far[p])
        def _():
            bx_second(p).wait_recv()
            bx_third(p).start()

    @pl.when(crossed)
    def _():
        for p in range(spread):
            bx_third(p).wait_recv()
        out_ref[...] = out_ref[...] + v["gtm_in"][...]

    @pl.when(is1)
    def _():
        pe_copy(z).wait_recv()
        out_ref[...] = part[z] + v["sib_part"][z]
        for c in range(CH):
            r = pl.ds(c * piece, piece)

            @pl.when(has_prev)
            def _():
                cr_copy(z, c).wait_recv()
                out_ref[r, :] = out_ref[r, :] + v["rsum"][z, r, :]

            @pl.when(z > 0)
            def _():
                fi_copy(c).wait_recv()
                out_ref[r, :] = out_ref[r, :] + fin[r, :]

    @pl.when(is1)
    def _():
        own_copy(0).wait_send()
        own_copy(1).wait_send()

    @pl.when(jnp.logical_and(is0, has_prev))
    def _():
        for c in range(CH):
            fi_copy(c).wait_send()

    pl.when(feeds)(lambda: tm_copy().wait_send())
    pl.when(fed)(lambda: gt_copy().wait_send())
    for p in range(spread):

        @pl.when(crossed)
        def _():
            fx_first(p).wait_send()

        @pl.when(cross)
        def _():
            bx_first(p).wait_send()

        @pl.when(tm == near[p])
        def _():
            fx_third(p).wait_send()
            bx_second(p).wait_send()

        if p:

            @pl.when(tm == far[p])
            def _():
                fx_second(p).wait_send()
                bx_third(p).wait_send()

    @pl.when(active)
    def _():
        for k in range(4):
            mx_send(k).wait_send()
        for k in range(6):
            gx_copy(k).wait_send()

    def drain(i, carry):
        b = blk(i)
        pl.when(jnp.where(is0, b <= z, b > z))(lambda: pe_copy(b).wait_send())
        pl.when(i < place)(lambda: sib_copy(b).wait_send())
        for c in range(CH):
            pl.when(jnp.logical_and(has_next, i <= place))(lambda: zr_copy(place - i, c, b).wait_send())
            pl.when(i > place)(lambda: cr_copy(b, c).wait_send())
        return carry

    lax.fori_loop(0, nz, drain, 0)


def local(dims, particles, source_pots, target_pots):
    times, nx, nz, rows, feats = dims
    half = rows // 2
    spread = times // 4
    dma = pltpu.SemaphoreType.DMA
    shapes = [
        ((nz, rows + 16, feats), F32),
        ((nx, rows + 16, feats), F32),
        ((nx * rows, feats), BF16),
        ((nx * rows, feats), BF16),
        ((8, nx * rows), F32),
        ((nz, rows, feats), F32),
        ((nz, rows, feats), F32),
        ((nz, rows, feats), F32),
        ((feats, nx * rows), F32),
        ((8, nx * rows), F32),
        ((nx, rows, feats), F32),
        ((2, rows, feats), F32),
        ((2, half, feats), F32),
        ((rows, feats), F32),
        ((rows, feats), F32),
        ((half // 2 + 8, feats), F32),
        ((rows // spread, feats), F32),
        ((rows, feats), BF16),
        ((rows, feats), BF16),
        ((feats, rows), BF16),
        ((feats, rows), BF16),
        ((rows, half), F32),
    ]
    scratch = [pltpu.VMEM(shape, kind) for shape, kind in shapes]
    line = nz * CH
    for count in (2, line, nz, 0, 4, nz, line, 6, 0, CH, spread, spread):
        kind = dma((count,)) if count else dma
        scratch += [kind, kind]
    out = pl.pallas_call(
        functools.partial(kernel, dims),
        out_shape=jax.ShapeDtypeStruct((rows, feats), F32),
        in_specs=[pl.BlockSpec(memory_space=pltpu.VMEM)] * 3,
        out_specs=pl.BlockSpec(memory_space=pltpu.VMEM),
        scratch_shapes=scratch,
        compiler_params=pltpu.CompilerParams(
            collective_id=0, has_side_effects=True, vmem_limit_bytes=56 * 2**20
        ),
    )(particles[0], source_pots, target_pots)
    return out[None]


def solution(mesh):
    times, nx, nz = mesh.shape["tm"], mesh.shape["row"], mesh.shape["col"]

    def program(particles, source_pots, target_pots):
        rows = particles.shape[1] // (nx * nz)
        dims = (times, nx, nz, rows, particles.shape[2])
        return jax.shard_map(
            functools.partial(local, dims),
            mesh=mesh,
            in_specs=(P("tm", ("row", "col"), None), P("tm", ("row", "col")), P("tm", ("row", "col"))),
            out_specs=P("tm", ("row", "col"), None),
            check_vma=False,
        )(particles, source_pots, target_pots)

    return program
```

```python
import functools
import math

import jax
import jax.numpy as jnp
from jax import lax
from jax.experimental import pallas as pl
from jax.experimental.pallas import tpu as pltpu
from jax.sharding import PartitionSpec as P

EPS = 0.1
MESH = pl.DeviceIdType.MESH
F32 = jnp.float32
BF16 = jnp.bfloat16


def split(x):
    hi = x.astype(BF16)
    return hi, (x - hi.astype(F32)).astype(BF16)


def dot(a, b, dims):
    return lax.dot_general(a, b, (dims, ((), ())), preferred_element_type=F32)


def dot3(a, b, dims):
    return dot(a[0], b[0], dims) + dot(a[0], b[1], dims) + dot(a[1], b[0], dims)


def eye(n):
    return lax.broadcasted_iota(jnp.int32, (n, n), 0) == lax.broadcasted_iota(jnp.int32, (n, n), 1)


def to_row(col):
    n = col.shape[0]
    return jnp.sum(jnp.where(eye(n), col, 0.0), axis=0, keepdims=True)


def to_col(row):
    n = row.shape[1]
    return jnp.sum(jnp.where(eye(n), row, 0.0), axis=1, keepdims=True)


BUFS = (
    "sbuf", "mbuf", "mhi", "mlo", "brow", "part", "sib_part", "rsum", "gmt", "csum", "gm",
    "gx_in", "gmid", "gtm_in", "fin", "relay", "back", "shi", "slo", "thi", "tlo", "acol",
)
SEMS = (
    "own", "zr", "sib", "tm", "mx", "pe", "cr", "gx", "gt", "fi",
    "fx", "bx",
)
CH = 4


def kernel(dims, pts_ref, spot_ref, tpot_ref, out_ref, *scratch):
    times, nx, nz, rows, feats = dims
    half = rows // 2
    hrow = half + 8
    piece = rows // CH
    last = nz - 1
    run = nz // 2
    mid = times // 2
    spread = mid // 2
    population = rows * nx * nz
    scale = math.log2(math.e) / EPS
    v = dict(zip(BUFS, scratch))
    sems = {name: scratch[len(BUFS) + 2 * i : len(BUFS) + 2 * i + 2] for i, name in enumerate(SEMS)}
    sbuf, mbuf, part, gm, fin = v["sbuf"], v["mbuf"], v["part"], v["gm"], v["fin"]
    mhi, mlo, brow, gmt, csum = v["mhi"], v["mlo"], v["brow"], v["gmt"], v["csum"]
    gx_in = v["gx_in"]

    tm, x, z = lax.axis_index("tm"), lax.axis_index("row"), lax.axis_index("col")
    core = lax.rem(tm, 2)
    is0, is1 = core == 0, core == 1
    active = tm < times - 1
    cross = tm == mid - 1
    crossed = tm == mid
    fed = jnp.logical_and(jnp.logical_and(is1, active), jnp.logical_not(cross))
    feeds = jnp.logical_and(jnp.logical_and(is0, tm > 0), jnp.logical_not(crossed))
    place = jnp.where(is0, z, last - z)
    has_prev, has_next = place > 0, place < last
    way = 1 - 2 * core
    forth = (tm, x, jnp.clip(z + way, 0, last))
    back_to = (tm, x, jnp.clip(z - way, 0, last))
    sib = (tm + 1 - 2 * core, x, z)
    before, after = (jnp.maximum(tm - 1, 0), x, z), (jnp.minimum(tm + 1, times - 1), x, z)
    x1, x2, x3 = lax.rem(x + 1, nx), lax.rem(x + 2, nx), lax.rem(x + 3, nx)
    xright, xleft = (tm, x1, z), (tm, x3, z)

    def at_time(t):
        return (t, x, z)

    def rdma(src, dst, name, to, k=None):
        s, r = sems[name]
        if k is not None:
            s, r = s.at[k], r.at[k]
        return pltpu.make_async_remote_copy(
            src_ref=src, dst_ref=dst, send_sem=s, recv_sem=r, device_id=to, device_id_type=MESH
        )

    barrier = pltpu.get_barrier_semaphore()

    def greet(to):
        pl.semaphore_signal(barrier, inc=1, device_id=to, device_id_type=MESH)

    for to in (sib, xright, xleft):
        greet(to)
    pl.when(has_prev)(lambda: greet(back_to))
    pl.when(feeds)(lambda: greet(before))
    pl.when(fed)(lambda: greet(after))
    partners = 3 + has_next.astype(jnp.int32)
    partners = partners + feeds.astype(jnp.int32) + fed.astype(jnp.int32)
    far = [mid + 2 * p for p in range(spread)]
    near = [2 * p for p in range(spread)]
    for p in range(spread):
        pl.when(cross)(lambda: greet(at_time(near[p])))
        pl.when(tm == near[p])(lambda: greet(at_time(far[p] if p else mid)))
        if p:
            pl.when(tm == far[p])(lambda: greet(at_time(mid)))

    relaying = jnp.logical_and(is0, jnp.logical_not(crossed))
    partners = partners + jnp.where(crossed, spread, relaying.astype(jnp.int32))

    pts = pts_ref[...]
    norm = to_row(jnp.sum(pts * pts, axis=1, keepdims=True)) * (scale / feats)
    trow = tpot_ref[...] * scale - norm
    srow = spot_ref[...] * scale - norm - math.log2(population)

    def put(buf, b):
        for i in range(2):
            buf[b, i * hrow : i * hrow + half, :] = pts[i * half : (i + 1) * half]
            pair = jnp.concatenate(
                [trow[:, i * half : (i + 1) * half], srow[:, i * half : (i + 1) * half], jnp.zeros((6, half), F32)], axis=0
            )
            buf[b, i * hrow + half : (i + 1) * hrow, :] = jnp.concatenate(
                [pair, jnp.zeros((8, feats - half), F32)], axis=1
            )

    pl.when(is0)(lambda: put(mbuf, x))
    pl.when(is1)(lambda: put(sbuf, z))

    pl.semaphore_wait(barrier, partners)

    def chunk(g, k):
        return pl.ds(pl.multiple_of(g * hrow + k * (half // 2), 8), half // 2 + 8 * k)

    def blk(i):
        return jnp.where(is0, i, last - i)

    def own_copy(i):
        ref = sbuf.at[z, pl.ds(i * hrow, hrow)]
        return rdma(ref, ref, "own", sib, i)

    def tm_copy():
        return rdma(mbuf.at[x], mbuf.at[x], "tm", before)

    h0, h1 = pl.ds(0, hrow), pl.ds(hrow, hrow)

    def mx_send(k):
        if k < 2:
            ref = mbuf.at[x]
        else:
            ref = mbuf.at[x3, h0] if k == 2 else mbuf.at[x1, h1]
        return rdma(ref, ref, "mx", xright if k % 2 == 0 else xleft, k)

    def mx_arrival(k):
        if k < 2:
            ref = mbuf.at[x3] if k == 0 else mbuf.at[x1]
        else:
            ref = mbuf.at[x2, h0] if k == 2 else mbuf.at[x2, h1]
        return rdma(ref, ref, "mx", xright, k)

    pieces = []
    for i in range(2):
        at = i * hrow
        pieces += [(at, half // 2), (at + half // 2, half // 2 + 8)]

    def fx_first(p):
        at, size = pieces[p]
        dst = v["relay"].at[pl.ds(0, size)]
        return rdma(mbuf.at[x, pl.ds(at, size)], dst, "fx", at_time(far[p] if p else near[p]), p)

    def fx_second(p):
        ref = v["relay"].at[pl.ds(0, pieces[p][1])]
        return rdma(ref, ref, "fx", at_time(near[p]), p)

    def fx_third(p):
        at, size = pieces[p]
        src = v["relay"].at[pl.ds(0, size)]
        return rdma(src, mbuf.at[x, pl.ds(at, size)], "fx", at_time(mid - 1), p)

    quarter = rows // spread

    def bx_first(p):
        return rdma(gm.at[x, pl.ds(p * quarter, quarter)], v["back"], "bx", at_time(near[p]), p)

    def bx_second(p):
        dst = v["back"] if p else v["gtm_in"].at[pl.ds(0, quarter)]
        return rdma(v["back"], dst, "bx", at_time(far[p] if p else mid), p)

    def bx_third(p):
        return rdma(v["back"], v["gtm_in"].at[pl.ds(p * quarter, quarter)], "bx", at_time(mid), p)

    def zr_part(s, g, k, b):
        ref = sbuf.at[b, chunk(g, k)]
        return rdma(ref, ref, "zr", forth, s * CH + 2 * g + k)

    def zr_copy(s, c, b):
        return zr_part(s, c // 2, c % 2, b)

    def sib_copy(b):
        return rdma(sbuf.at[b], sbuf.at[b], "sib", sib, b)

    @pl.when(is1)
    def _():
        own_copy(0).start()
        own_copy(1).start()
        for c in range(CH):
            pl.when(has_next)(lambda: zr_copy(0, c, z).start())

    @pl.when(is0)
    def _():
        pl.when(feeds)(lambda: tm_copy().start())

        @pl.when(crossed)
        def _():
            for p in range(spread):
                fx_first(p).start()

        mx_send(0).start()
        mx_send(1).start()
        for i in range(2):
            own_copy(i).wait_recv()
            for c in (2 * i, 2 * i + 1):
                pl.when(has_next)(lambda: zr_copy(0, c, z).start())

    chain_at = nz + 1
    near_at, far_at, back_at = run, 1, 15
    wait_m = jnp.where(cross, run + 1, 1)
    mx_step = jnp.where(cross, run + 2, jnp.where(is0, 1, 3))
    first = jnp.where(cross, nz - 1, jnp.where(is0, 3, 4))
    pace = jnp.where(cross, 2, 1)
    ahead = (nz - first) * pace

    def order(n):
        k = jnp.where(n < ahead, last - n, n - ahead)
        low = jnp.minimum(z, last - z)
        single = last - 2 * low
        d = (k - single) // 2
        b = jnp.where(k < single, last - k, jnp.where(lax.rem(k - single, 2) == 0, 2 * low - d, d))
        return jnp.where(z < nz - nz // 2, b, last - b)

    def pe_copy(b):
        return rdma(part.at[b], v["sib_part"].at[b], "pe", sib, b)

    def prepare():
        mx_arrival(2).wait_recv()
        mx_arrival(3).wait_recv()
        for j in range(nx):
            for i in range(2):
                at = j * rows + i * half
                hi, lo = split(mbuf[j, i * hrow : i * hrow + half, :])
                mhi[at : at + half, :] = hi
                mlo[at : at + half, :] = lo
                pair = mbuf[j, i * hrow + half : (i + 1) * hrow, 0:half]
                brow[0:1, at : at + half] = jnp.where(is0, pair[1:2], pair[0:1])

    def tile_open(b):
        for i in range(2):
            at = slice(i * half, (i + 1) * half)
            s = sbuf[b, i * hrow : i * hrow + half, :]
            hi, lo = split(s)
            v["shi"][at, :] = hi
            v["slo"][at, :] = lo
            hi, lo = split(s.T)
            v["thi"][:, at] = hi
            v["tlo"][:, at] = lo
            pair = sbuf[b, i * hrow + half : (i + 1) * hrow, 0:half]
            v["acol"][at, :] = jnp.broadcast_to(to_col(jnp.where(is0, pair[0:1], pair[1:2])), (half, half))

    def tile_part(b, c):
        width = nx * rows // 2
        at = pl.ds(pl.multiple_of(c * width, width), width)
        m = (mhi[at, :], mlo[at, :])
        g = dot3((v["shi"][...], v["slo"][...]), m, ((1,), (1,)))
        w = jnp.exp2(g * (2.0 * scale / feats) + v["acol"][:, 0:1] + brow[0:1, at])
        total = jnp.sum(w, axis=1, keepdims=True)
        csum[0:1, at] += jnp.sum(w, axis=0, keepdims=True)
        ww = split(w)
        moved = dot3(ww, m, ((1,), (0,)))
        gmt[:, at] += dot3((v["thi"][...], v["tlo"][...]), ww, ((1,), (0,)))
        for i in range(2):
            r = slice(i * half, (i + 1) * half)
            part[b, r, :] = part[b, r, :] + (total[r] * sbuf[b, i * hrow : i * hrow + half, :] - moved[r])

    gmt[...] = jnp.zeros_like(gmt)
    csum[...] = jnp.zeros_like(csum)

    g0, g1 = pl.ds(0, half), pl.ds(half, half)

    def gx_copy(k):
        src, dst = [
            (gm.at[x2, g0], v["gmid"].at[0]),
            (gm.at[x2, g1], v["gmid"].at[1]),
            (gm.at[x1, g1], gx_in.at[0, g1]),
            (gm.at[x3, g0], gx_in.at[1, g0]),
            (gm.at[x1, g0], gx_in.at[0, g0]),
            (gm.at[x3, g1], gx_in.at[1, g1]),
        ][k]
        return rdma(src, dst, "gx", xright if k % 2 == 0 else xleft, k)

    def finish_m(j):
        at = pl.ds(pl.multiple_of(j * rows, rows), rows)
        ccol = to_col(csum[0:1, at])
        g = gmt[:, at].T
        for i in range(2):
            lo = i * half
            gm[j, lo : lo + half, :] = ccol[lo : lo + half] * mbuf[j, i * hrow : i * hrow + half, :] - g[lo : lo + half]

    def gt_copy():
        return rdma(gm.at[x], v["gtm_in"], "gt", after)

    def cr_copy(b, c):
        ref = v["rsum"].at[b, pl.ds(c * piece, piece)]
        return rdma(ref, ref, "cr", forth, b * CH + c)

    def fi_copy(c):
        r = pl.ds(c * piece, piece)
        return rdma(v["rsum"].at[z, r], fin.at[r], "fi", sib, c)

    def step(s, carry):
        @pl.when(jnp.logical_and(is0, s == back_at))
        def _():
            for p in range(spread):

                @pl.when(tm == near[p])
                def _():
                    bx_first(p).wait_recv()
                    bx_second(p).start()

        @pl.when(jnp.logical_and(is0, jnp.logical_or(s == far_at, s == near_at)))
        def _():
            for p in range(1, spread):

                @pl.when(jnp.logical_and(s == far_at, tm == far[p]))
                def _():
                    fx_second(p).wait_recv()
                    fx_second(p).start()

            for p in range(spread):

                @pl.when(jnp.logical_and(s == near_at, tm == near[p]))
                def _():
                    fx_second(p).wait_recv()
                    fx_third(p).start()

        @pl.when(s <= first)
        def _():
            @pl.when(s == wait_m)
            def _():
                @pl.when(fed)
                def _():
                    tm_copy().wait_recv()

                @pl.when(cross)
                def _():
                    for p in range(spread):
                        at, size = pieces[p]
                        ref = mbuf.at[x, pl.ds(at, size)]
                        rdma(ref, ref, "fx", at_time(mid - 1), p).wait_recv()

                @pl.when(jnp.logical_or(fed, cross))
                def _():
                    mx_send(0).start()
                    mx_send(1).start()

            @pl.when(jnp.logical_and(active, s == mx_step))
            def _():
                mx_arrival(0).wait_recv()
                mx_send(2).start()
                mx_arrival(1).wait_recv()
                mx_send(3).start()

            pl.when(jnp.logical_and(active, s == first))(prepare)

        relays = jnp.logical_and(s <= last, s <= place)
        onward = jnp.logical_and(relays, jnp.logical_and(has_next, s < last))
        at = blk(place - s)

        def unit(u, carry):
            c = lax.rem(u, 2)
            n = (s - first) * pace + u // 2
            b = order(jnp.clip(n, 0, last))
            has_tile = jnp.logical_and(n >= 0, n < nz)

            @pl.when(jnp.logical_and(relays, u < 2))
            def _():
                for k in range(2):
                    zr_part(s - 1, u, k, at).wait_recv()
                    pl.when(onward)(lambda: zr_part(s, u, k, at).start())

            @pl.when(has_tile)
            def _():
                @pl.when(c == 0)
                def _():
                    pl.when(jnp.where(is0, b > z, b < z))(lambda: sib_copy(b).wait_recv())
                    part[b] = jnp.zeros((rows, feats), F32)
                    pl.when(active)(lambda: tile_open(b))

                pl.when(active)(lambda: tile_part(b, c))

                @pl.when(jnp.logical_and(c == 1, jnp.where(is0, b <= z, b > z)))
                def _():
                    pe_copy(b).start()

            return carry

        units = jnp.where(jnp.logical_or(s <= last, s < first + nz // pace), 2 * jnp.where(s < first, 1, pace), 0)
        lax.fori_loop(0, units, unit, 0)
        pl.when(relays)(lambda: sib_copy(at).start())

        cs = s - chain_at

        @pl.when(jnp.logical_and(jnp.logical_and(cs >= place, cs < last), has_next))
        def _():
            t = blk(last - cs + place)
            pe_copy(t).wait_recv()
            for c in range(CH):
                r = pl.ds(c * piece, piece)

                @pl.when(has_prev)
                def _():
                    cr_copy(t, c).wait_recv()
                    v["rsum"][t, r, :] = v["rsum"][t, r, :] + (part[t, r, :] + v["sib_part"][t, r, :])

                @pl.when(jnp.logical_not(has_prev))
                def _():
                    v["rsum"][t, r, :] = part[t, r, :] + v["sib_part"][t, r, :]

                cr_copy(t, c).start()

        done = s - first - nz // pace

        @pl.when(jnp.logical_and(active, done >= 0))
        def _():
            @pl.when(done == 0)
            def _():
                finish_m(x2)
                gx_copy(0).start()
                gx_copy(1).start()
                finish_m(x1)
                gx_copy(2).start()
                finish_m(x3)
                gx_copy(3).start()
                finish_m(x)

            @pl.when(done == 1)
            def _():
                gx_copy(0).wait_recv()
                gm[x1, g0, :] = gm[x1, g0, :] + v["gmid"][0]
                gx_copy(4).start()
                gx_copy(1).wait_recv()
                gm[x3, g1, :] = gm[x3, g1, :] + v["gmid"][1]
                gx_copy(5).start()

            @pl.when(done == 2)
            def _():
                for k in range(2, 6):
                    gx_copy(k).wait_recv()
                gm[x] = gm[x] + gx_in[0] + gx_in[1]
                pl.when(fed)(lambda: gt_copy().start())

                @pl.when(cross)
                def _():
                    for p in range(spread):
                        bx_first(p).start()

        return carry

    steps = jnp.maximum(first + nz // pace + 3, chain_at + last)
    lax.fori_loop(1, steps, step, 0)

    @pl.when(is0)
    def _():
        @pl.when(has_prev)
        def _():
            for c in range(CH):
                cr_copy(z, c).wait_recv()
                fi_copy(c).start()

        out_ref[...] = gm[x]

        @pl.when(feeds)
        def _():
            gt_copy().wait_recv()
            out_ref[...] = out_ref[...] + v["gtm_in"][...]

    for p in range(1, spread):

        @pl.when(tm == far[p])
        def _():
            bx_second(p).wait_recv()
            bx_third(p).start()

    @pl.when(crossed)
    def _():
        for p in range(spread):
            bx_third(p).wait_recv()
        out_ref[...] = out_ref[...] + v["gtm_in"][...]

    @pl.when(is1)
    def _():
        pe_copy(z).wait_recv()
        out_ref[...] = part[z] + v["sib_part"][z]
        for c in range(CH):
            r = pl.ds(c * piece, piece)

            @pl.when(has_prev)
            def _():
                cr_copy(z, c).wait_recv()
                out_ref[r, :] = out_ref[r, :] + v["rsum"][z, r, :]

            @pl.when(z > 0)
            def _():
                fi_copy(c).wait_recv()
                out_ref[r, :] = out_ref[r, :] + fin[r, :]

    @pl.when(is1)
    def _():
        own_copy(0).wait_send()
        own_copy(1).wait_send()

    @pl.when(jnp.logical_and(is0, has_prev))
    def _():
        for c in range(CH):
            fi_copy(c).wait_send()

    pl.when(feeds)(lambda: tm_copy().wait_send())
    pl.when(fed)(lambda: gt_copy().wait_send())
    for p in range(spread):

        @pl.when(crossed)
        def _():
            fx_first(p).wait_send()

        @pl.when(cross)
        def _():
            bx_first(p).wait_send()

        @pl.when(tm == near[p])
        def _():
            fx_third(p).wait_send()
            bx_second(p).wait_send()

        if p:

            @pl.when(tm == far[p])
            def _():
                fx_second(p).wait_send()
                bx_third(p).wait_send()

    @pl.when(active)
    def _():
        for k in range(4):
            mx_send(k).wait_send()
        for k in range(6):
            gx_copy(k).wait_send()

    def drain(i, carry):
        b = blk(i)
        pl.when(jnp.where(is0, b <= z, b > z))(lambda: pe_copy(b).wait_send())
        pl.when(i < place)(lambda: sib_copy(b).wait_send())
        for c in range(CH):
            pl.when(jnp.logical_and(has_next, i <= place))(lambda: zr_copy(place - i, c, b).wait_send())
            pl.when(i > place)(lambda: cr_copy(b, c).wait_send())
        return carry

    lax.fori_loop(0, nz, drain, 0)


def local(dims, particles, source_pots, target_pots):
    times, nx, nz, rows, feats = dims
    half = rows // 2
    spread = times // 4
    dma = pltpu.SemaphoreType.DMA
    shapes = [
        ((nz, rows + 16, feats), F32),
        ((nx, rows + 16, feats), F32),
        ((nx * rows, feats), BF16),
        ((nx * rows, feats), BF16),
        ((8, nx * rows), F32),
        ((nz, rows, feats), F32),
        ((nz, rows, feats), F32),
        ((nz, rows, feats), F32),
        ((feats, nx * rows), F32),
        ((8, nx * rows), F32),
        ((nx, rows, feats), F32),
        ((2, rows, feats), F32),
        ((2, half, feats), F32),
        ((rows, feats), F32),
        ((rows, feats), F32),
        ((half // 2 + 8, feats), F32),
        ((rows // spread, feats), F32),
        ((rows, feats), BF16),
        ((rows, feats), BF16),
        ((feats, rows), BF16),
        ((feats, rows), BF16),
        ((rows, half), F32),
    ]
    scratch = [pltpu.VMEM(shape, kind) for shape, kind in shapes]
    line = nz * CH
    for count in (2, line, nz, 0, 4, nz, line, 6, 0, CH, spread, spread):
        kind = dma((count,)) if count else dma
        scratch += [kind, kind]
    out = pl.pallas_call(
        functools.partial(kernel, dims),
        out_shape=jax.ShapeDtypeStruct((rows, feats), F32),
        in_specs=[pl.BlockSpec(memory_space=pltpu.VMEM)] * 3,
        out_specs=pl.BlockSpec(memory_space=pltpu.VMEM),
        scratch_shapes=scratch,
        compiler_params=pltpu.CompilerParams(
            collective_id=0, has_side_effects=True, vmem_limit_bytes=56 * 2**20
        ),
    )(particles[0], source_pots, target_pots)
    return out[None]


def solution(mesh):
    times, nx, nz = mesh.shape["tm"], mesh.shape["row"], mesh.shape["col"]

    def program(particles, source_pots, target_pots):
        rows = particles.shape[1] // (nx * nz)
        dims = (times, nx, nz, rows, particles.shape[2])
        return jax.shard_map(
            functools.partial(local, dims),
            mesh=mesh,
            in_specs=(P("tm", ("row", "col"), None), P("tm", ("row", "col")), P("tm", ("row", "col"))),
            out_specs=P("tm", ("row", "col"), None),
            check_vma=False,
        )(particles, source_pots, target_pots)

    return program
```

```python
import functools
import math

import jax
import jax.numpy as jnp
from jax import lax
from jax.experimental import pallas as pl
from jax.experimental.pallas import tpu as pltpu
from jax.sharding import PartitionSpec as P

EPS = 0.1
MESH = pl.DeviceIdType.MESH
F32 = jnp.float32
BF16 = jnp.bfloat16


def split(x):
    hi = x.astype(BF16)
    return hi, (x - hi.astype(F32)).astype(BF16)


def dot(a, b, dims):
    return lax.dot_general(a, b, (dims, ((), ())), preferred_element_type=F32)


def dot3(a, b, dims):
    return dot(a[0], b[0], dims) + dot(a[0], b[1], dims) + dot(a[1], b[0], dims)


def eye(n):
    return lax.broadcasted_iota(jnp.int32, (n, n), 0) == lax.broadcasted_iota(jnp.int32, (n, n), 1)


def to_row(col):
    n = col.shape[0]
    return jnp.sum(jnp.where(eye(n), col, 0.0), axis=0, keepdims=True)


def to_col(row):
    n = row.shape[1]
    return jnp.sum(jnp.where(eye(n), row, 0.0), axis=1, keepdims=True)


BUFS = (
    "sbuf", "mbuf", "mhi", "mlo", "brow", "part", "sib_part", "rsum", "gmt", "csum", "gm",
    "gx_in", "gmid", "gtm_in", "fin", "relay", "back", "shi", "slo", "thi", "tlo", "acol",
)
SEMS = (
    "own", "zr", "sib", "tm", "mx", "pe", "cr", "gx", "gt", "fi",
    "fx", "bx",
)
CH = 4


def kernel(dims, pts_ref, spot_ref, tpot_ref, out_ref, *scratch):
    times, nx, nz, rows, feats = dims
    half = rows // 2
    hrow = half + 8
    piece = rows // CH
    last = nz - 1
    run = nz // 2
    mid = times // 2
    spread = mid // 2
    population = rows * nx * nz
    scale = math.log2(math.e) / EPS
    v = dict(zip(BUFS, scratch))
    sems = {name: scratch[len(BUFS) + 2 * i : len(BUFS) + 2 * i + 2] for i, name in enumerate(SEMS)}
    sbuf, mbuf, part, gm, fin = v["sbuf"], v["mbuf"], v["part"], v["gm"], v["fin"]
    mhi, mlo, brow, gmt, csum = v["mhi"], v["mlo"], v["brow"], v["gmt"], v["csum"]
    gx_in = v["gx_in"]

    tm, x, z = lax.axis_index("tm"), lax.axis_index("row"), lax.axis_index("col")
    core = lax.rem(tm, 2)
    is0, is1 = core == 0, core == 1
    active = tm < times - 1
    cross = tm == mid - 1
    crossed = tm == mid
    fed = jnp.logical_and(jnp.logical_and(is1, active), jnp.logical_not(cross))
    feeds = jnp.logical_and(jnp.logical_and(is0, tm > 0), jnp.logical_not(crossed))
    place = jnp.where(is0, z, last - z)
    has_prev, has_next = place > 0, place < last
    way = 1 - 2 * core
    forth = (tm, x, jnp.clip(z + way, 0, last))
    back_to = (tm, x, jnp.clip(z - way, 0, last))
    sib = (tm + 1 - 2 * core, x, z)
    before, after = (jnp.maximum(tm - 1, 0), x, z), (jnp.minimum(tm + 1, times - 1), x, z)
    x1, x2, x3 = lax.rem(x + 1, nx), lax.rem(x + 2, nx), lax.rem(x + 3, nx)
    xright, xleft = (tm, x1, z), (tm, x3, z)

    def at_time(t):
        return (t, x, z)

    def rdma(src, dst, name, to, k=None):
        s, r = sems[name]
        if k is not None:
            s, r = s.at[k], r.at[k]
        return pltpu.make_async_remote_copy(
            src_ref=src, dst_ref=dst, send_sem=s, recv_sem=r, device_id=to, device_id_type=MESH
        )

    barrier = pltpu.get_barrier_semaphore()

    def greet(to):
        pl.semaphore_signal(barrier, inc=1, device_id=to, device_id_type=MESH)

    for to in (sib, xright, xleft):
        greet(to)
    pl.when(has_prev)(lambda: greet(back_to))
    pl.when(feeds)(lambda: greet(before))
    pl.when(fed)(lambda: greet(after))
    partners = 3 + has_next.astype(jnp.int32)
    partners = partners + feeds.astype(jnp.int32) + fed.astype(jnp.int32)
    far = [mid + 2 * p for p in range(spread)]
    near = [2 * p for p in range(spread)]
    for p in range(spread):
        pl.when(cross)(lambda: greet(at_time(near[p])))
        pl.when(tm == near[p])(lambda: greet(at_time(far[p] if p else mid)))
        if p:
            pl.when(tm == far[p])(lambda: greet(at_time(mid)))

    relaying = jnp.logical_and(is0, jnp.logical_not(crossed))
    partners = partners + jnp.where(crossed, spread, relaying.astype(jnp.int32))

    pts = pts_ref[...]
    norm = to_row(jnp.sum(pts * pts, axis=1, keepdims=True)) * (scale / feats)
    trow = tpot_ref[...] * scale - norm
    srow = spot_ref[...] * scale - norm - math.log2(population)

    def put(buf, b):
        for i in range(2):
            buf[b, i * hrow : i * hrow + half, :] = pts[i * half : (i + 1) * half]
            pair = jnp.concatenate(
                [trow[:, i * half : (i + 1) * half], srow[:, i * half : (i + 1) * half], jnp.zeros((6, half), F32)], axis=0
            )
            buf[b, i * hrow + half : (i + 1) * hrow, :] = jnp.concatenate(
                [pair, jnp.zeros((8, feats - half), F32)], axis=1
            )

    pl.when(is0)(lambda: put(mbuf, x))
    pl.when(is1)(lambda: put(sbuf, z))

    pl.semaphore_wait(barrier, partners)

    def chunk(g, k):
        return pl.ds(pl.multiple_of(g * hrow + k * (half // 2), 8), half // 2 + 8 * k)

    def blk(i):
        return jnp.where(is0, i, last - i)

    def own_copy(i):
        ref = sbuf.at[z, pl.ds(i * hrow, hrow)]
        return rdma(ref, ref, "own", sib, i)

    def tm_copy():
        return rdma(mbuf.at[x], mbuf.at[x], "tm", before)

    h0, h1 = pl.ds(0, hrow), pl.ds(hrow, hrow)

    def mx_send(k):
        if k < 2:
            ref = mbuf.at[x]
        else:
            ref = mbuf.at[x3, h0] if k == 2 else mbuf.at[x1, h1]
        return rdma(ref, ref, "mx", xright if k % 2 == 0 else xleft, k)

    def mx_arrival(k):
        if k < 2:
            ref = mbuf.at[x3] if k == 0 else mbuf.at[x1]
        else:
            ref = mbuf.at[x2, h0] if k == 2 else mbuf.at[x2, h1]
        return rdma(ref, ref, "mx", xright, k)

    pieces = []
    for i in range(2):
        at = i * hrow
        pieces += [(at, half // 2), (at + half // 2, half // 2 + 8)]

    def fx_first(p):
        at, size = pieces[p]
        dst = v["relay"].at[pl.ds(0, size)]
        return rdma(mbuf.at[x, pl.ds(at, size)], dst, "fx", at_time(far[p] if p else near[p]), p)

    def fx_second(p):
        ref = v["relay"].at[pl.ds(0, pieces[p][1])]
        return rdma(ref, ref, "fx", at_time(near[p]), p)

    def fx_third(p):
        at, size = pieces[p]
        src = v["relay"].at[pl.ds(0, size)]
        return rdma(src, mbuf.at[x, pl.ds(at, size)], "fx", at_time(mid - 1), p)

    quarter = rows // spread

    def bx_first(p):
        return rdma(gm.at[x, pl.ds(p * quarter, quarter)], v["back"], "bx", at_time(near[p]), p)

    def bx_second(p):
        dst = v["back"] if p else v["gtm_in"].at[pl.ds(0, quarter)]
        return rdma(v["back"], dst, "bx", at_time(far[p] if p else mid), p)

    def bx_third(p):
        return rdma(v["back"], v["gtm_in"].at[pl.ds(p * quarter, quarter)], "bx", at_time(mid), p)

    def zr_part(s, g, k, b):
        ref = sbuf.at[b, chunk(g, k)]
        return rdma(ref, ref, "zr", forth, s * CH + 2 * g + k)

    def zr_copy(s, c, b):
        return zr_part(s, c // 2, c % 2, b)

    def sib_copy(b):
        return rdma(sbuf.at[b], sbuf.at[b], "sib", sib, b)

    @pl.when(is1)
    def _():
        own_copy(0).start()
        own_copy(1).start()
        for c in range(CH):
            pl.when(has_next)(lambda: zr_copy(0, c, z).start())

    @pl.when(is0)
    def _():
        pl.when(feeds)(lambda: tm_copy().start())

        @pl.when(crossed)
        def _():
            for p in range(spread):
                fx_first(p).start()

        mx_send(0).start()
        mx_send(1).start()
        for i in range(2):
            own_copy(i).wait_recv()
            for c in (2 * i, 2 * i + 1):
                pl.when(has_next)(lambda: zr_copy(0, c, z).start())

    chain_at = nz
    near_at, far_at, back_at = run, 1, 14
    wait_m = jnp.where(cross, run + 1, 1)
    mx_step = jnp.where(cross, run + 2, jnp.where(is0, 1, 3))
    first = jnp.where(cross, nz - 1, jnp.where(is0, 3, 4))
    pace = jnp.where(cross, 2, 1)
    ahead = (nz - first) * pace

    def order(n):
        k = jnp.where(n < ahead, last - n, n - ahead)
        low = jnp.minimum(z, last - z)
        single = last - 2 * low
        d = (k - single) // 2
        b = jnp.where(k < single, last - k, jnp.where(lax.rem(k - single, 2) == 0, 2 * low - d, d))
        return jnp.where(z < nz - nz // 2, b, last - b)

    def pe_copy(b):
        return rdma(part.at[b], v["sib_part"].at[b], "pe", sib, b)

    def prepare():
        mx_arrival(2).wait_recv()
        mx_arrival(3).wait_recv()
        for j in range(nx):
            for i in range(2):
                at = j * rows + i * half
                hi, lo = split(mbuf[j, i * hrow : i * hrow + half, :])
                mhi[at : at + half, :] = hi
                mlo[at : at + half, :] = lo
                pair = mbuf[j, i * hrow + half : (i + 1) * hrow, 0:half]
                brow[0:1, at : at + half] = jnp.where(is0, pair[1:2], pair[0:1])

    def tile_open(b):
        for i in range(2):
            at = slice(i * half, (i + 1) * half)
            s = sbuf[b, i * hrow : i * hrow + half, :]
            hi, lo = split(s)
            v["shi"][at, :] = hi
            v["slo"][at, :] = lo
            hi, lo = split(s.T)
            v["thi"][:, at] = hi
            v["tlo"][:, at] = lo
            pair = sbuf[b, i * hrow + half : (i + 1) * hrow, 0:half]
            v["acol"][at, :] = jnp.broadcast_to(to_col(jnp.where(is0, pair[0:1], pair[1:2])), (half, half))

    def tile_part(b, c):
        width = nx * rows // 2
        at = pl.ds(pl.multiple_of(c * width, width), width)
        m = (mhi[at, :], mlo[at, :])
        g = dot3((v["shi"][...], v["slo"][...]), m, ((1,), (1,)))
        w = jnp.exp2(g * (2.0 * scale / feats) + v["acol"][:, 0:1] + brow[0:1, at])
        total = jnp.sum(w, axis=1, keepdims=True)
        csum[0:1, at] += jnp.sum(w, axis=0, keepdims=True)
        ww = split(w)
        moved = dot3(ww, m, ((1,), (0,)))
        gmt[:, at] += dot3((v["thi"][...], v["tlo"][...]), ww, ((1,), (0,)))
        for i in range(2):
            r = slice(i * half, (i + 1) * half)
            part[b, r, :] = part[b, r, :] + (total[r] * sbuf[b, i * hrow : i * hrow + half, :] - moved[r])

    gmt[...] = jnp.zeros_like(gmt)
    csum[...] = jnp.zeros_like(csum)

    g0, g1 = pl.ds(0, half), pl.ds(half, half)

    def gx_copy(k):
        src, dst = [
            (gm.at[x2, g0], v["gmid"].at[0]),
            (gm.at[x2, g1], v["gmid"].at[1]),
            (gm.at[x1, g1], gx_in.at[0, g1]),
            (gm.at[x3, g0], gx_in.at[1, g0]),
            (gm.at[x1, g0], gx_in.at[0, g0]),
            (gm.at[x3, g1], gx_in.at[1, g1]),
        ][k]
        return rdma(src, dst, "gx", xright if k % 2 == 0 else xleft, k)

    def finish_m(j):
        at = pl.ds(pl.multiple_of(j * rows, rows), rows)
        ccol = to_col(csum[0:1, at])
        g = gmt[:, at].T
        for i in range(2):
            lo = i * half
            gm[j, lo : lo + half, :] = ccol[lo : lo + half] * mbuf[j, i * hrow : i * hrow + half, :] - g[lo : lo + half]

    def gt_copy():
        return rdma(gm.at[x], v["gtm_in"], "gt", after)

    def cr_copy(b, c):
        ref = v["rsum"].at[b, pl.ds(c * piece, piece)]
        return rdma(ref, ref, "cr", forth, b * CH + c)

    def fi_copy(c):
        r = pl.ds(c * piece, piece)
        return rdma(v["rsum"].at[z, r], fin.at[r], "fi", sib, c)

    def step(s, carry):
        @pl.when(jnp.logical_and(is0, s == back_at))
        def _():
            for p in range(spread):

                @pl.when(tm == near[p])
                def _():
                    bx_first(p).wait_recv()
                    bx_second(p).start()

        @pl.when(jnp.logical_and(is0, jnp.logical_or(s == far_at, s == near_at)))
        def _():
            for p in range(1, spread):

                @pl.when(jnp.logical_and(s == far_at, tm == far[p]))
                def _():
                    fx_second(p).wait_recv()
                    fx_second(p).start()

            for p in range(spread):

                @pl.when(jnp.logical_and(s == near_at, tm == near[p]))
                def _():
                    fx_second(p).wait_recv()
                    fx_third(p).start()

        @pl.when(s <= first)
        def _():
            @pl.when(s == wait_m)
            def _():
                @pl.when(fed)
                def _():
                    tm_copy().wait_recv()

                @pl.when(cross)
                def _():
                    for p in range(spread):
                        at, size = pieces[p]
                        ref = mbuf.at[x, pl.ds(at, size)]
                        rdma(ref, ref, "fx", at_time(mid - 1), p).wait_recv()

                @pl.when(jnp.logical_or(fed, cross))
                def _():
                    mx_send(0).start()
                    mx_send(1).start()

            @pl.when(jnp.logical_and(active, s == mx_step))
            def _():
                mx_arrival(0).wait_recv()
                mx_send(2).start()
                mx_arrival(1).wait_recv()
                mx_send(3).start()

            pl.when(jnp.logical_and(active, s == first))(prepare)

        relays = jnp.logical_and(s <= last, s <= place)
        onward = jnp.logical_and(relays, jnp.logical_and(has_next, s < last))
        at = blk(place - s)

        def unit(u, carry):
            c = lax.rem(u, 2)
            n = (s - first) * pace + u // 2
            b = order(jnp.clip(n, 0, last))
            has_tile = jnp.logical_and(n >= 0, n < nz)

            @pl.when(jnp.logical_and(relays, u < 2))
            def _():
                for k in range(2):
                    zr_part(s - 1, u, k, at).wait_recv()
                    pl.when(onward)(lambda: zr_part(s, u, k, at).start())

            @pl.when(has_tile)
            def _():
                @pl.when(c == 0)
                def _():
                    pl.when(jnp.where(is0, b > z, b < z))(lambda: sib_copy(b).wait_recv())
                    part[b] = jnp.zeros((rows, feats), F32)
                    pl.when(active)(lambda: tile_open(b))

                pl.when(active)(lambda: tile_part(b, c))

                @pl.when(jnp.logical_and(c == 1, jnp.where(is0, b <= z, b > z)))
                def _():
                    pe_copy(b).start()

            return carry

        units = jnp.where(jnp.logical_or(s <= last, s < first + nz // pace), 2 * jnp.where(s < first, 1, pace), 0)
        lax.fori_loop(0, units, unit, 0)
        pl.when(relays)(lambda: sib_copy(at).start())

        cs = s - chain_at

        @pl.when(jnp.logical_and(jnp.logical_and(cs >= place, cs < last), has_next))
        def _():
            t = blk(last - cs + place)
            pe_copy(t).wait_recv()
            for c in range(CH):
                r = pl.ds(c * piece, piece)

                @pl.when(has_prev)
                def _():
                    cr_copy(t, c).wait_recv()
                    v["rsum"][t, r, :] = v["rsum"][t, r, :] + (part[t, r, :] + v["sib_part"][t, r, :])

                @pl.when(jnp.logical_not(has_prev))
                def _():
                    v["rsum"][t, r, :] = part[t, r, :] + v["sib_part"][t, r, :]

                cr_copy(t, c).start()

        done = s - first - nz // pace + 1

        @pl.when(jnp.logical_and(active, done >= 0))
        def _():
            @pl.when(done == 0)
            def _():
                finish_m(x2)
                gx_copy(0).start()
                gx_copy(1).start()
                finish_m(x1)
                gx_copy(2).start()
                finish_m(x3)
                gx_copy(3).start()
                finish_m(x)

            @pl.when(done == 1)
            def _():
                gx_copy(0).wait_recv()
                gm[x1, g0, :] = gm[x1, g0, :] + v["gmid"][0]
                gx_copy(4).start()
                gx_copy(1).wait_recv()
                gm[x3, g1, :] = gm[x3, g1, :] + v["gmid"][1]
                gx_copy(5).start()

            @pl.when(done == 2)
            def _():
                for k in range(2, 6):
                    gx_copy(k).wait_recv()
                gm[x] = gm[x] + gx_in[0] + gx_in[1]
                pl.when(fed)(lambda: gt_copy().start())

                @pl.when(cross)
                def _():
                    for p in range(spread):
                        bx_first(p).start()

        return carry

    steps = jnp.maximum(first + nz // pace + 3, chain_at + last)
    lax.fori_loop(1, steps, step, 0)

    @pl.when(is0)
    def _():
        @pl.when(has_prev)
        def _():
            for c in range(CH):
                cr_copy(z, c).wait_recv()
                fi_copy(c).start()

        out_ref[...] = gm[x]

        @pl.when(feeds)
        def _():
            gt_copy().wait_recv()
            out_ref[...] = out_ref[...] + v["gtm_in"][...]

    for p in range(1, spread):

        @pl.when(tm == far[p])
        def _():
            bx_second(p).wait_recv()
            bx_third(p).start()

    @pl.when(crossed)
    def _():
        for p in range(spread):
            bx_third(p).wait_recv()
        out_ref[...] = out_ref[...] + v["gtm_in"][...]

    @pl.when(is1)
    def _():
        pe_copy(z).wait_recv()
        out_ref[...] = part[z] + v["sib_part"][z]
        for c in range(CH):
            r = pl.ds(c * piece, piece)

            @pl.when(has_prev)
            def _():
                cr_copy(z, c).wait_recv()
                out_ref[r, :] = out_ref[r, :] + v["rsum"][z, r, :]

            @pl.when(z > 0)
            def _():
                fi_copy(c).wait_recv()
                out_ref[r, :] = out_ref[r, :] + fin[r, :]

    @pl.when(is1)
    def _():
        own_copy(0).wait_send()
        own_copy(1).wait_send()

    @pl.when(jnp.logical_and(is0, has_prev))
    def _():
        for c in range(CH):
            fi_copy(c).wait_send()

    pl.when(feeds)(lambda: tm_copy().wait_send())
    pl.when(fed)(lambda: gt_copy().wait_send())
    for p in range(spread):

        @pl.when(crossed)
        def _():
            fx_first(p).wait_send()

        @pl.when(cross)
        def _():
            bx_first(p).wait_send()

        @pl.when(tm == near[p])
        def _():
            fx_third(p).wait_send()
            bx_second(p).wait_send()

        if p:

            @pl.when(tm == far[p])
            def _():
                fx_second(p).wait_send()
                bx_third(p).wait_send()

    @pl.when(active)
    def _():
        for k in range(4):
            mx_send(k).wait_send()
        for k in range(6):
            gx_copy(k).wait_send()

    def drain(i, carry):
        b = blk(i)
        pl.when(jnp.where(is0, b <= z, b > z))(lambda: pe_copy(b).wait_send())
        pl.when(i < place)(lambda: sib_copy(b).wait_send())
        for c in range(CH):
            pl.when(jnp.logical_and(has_next, i <= place))(lambda: zr_copy(place - i, c, b).wait_send())
            pl.when(i > place)(lambda: cr_copy(b, c).wait_send())
        return carry

    lax.fori_loop(0, nz, drain, 0)


def local(dims, particles, source_pots, target_pots):
    times, nx, nz, rows, feats = dims
    half = rows // 2
    spread = times // 4
    dma = pltpu.SemaphoreType.DMA
    shapes = [
        ((nz, rows + 16, feats), F32),
        ((nx, rows + 16, feats), F32),
        ((nx * rows, feats), BF16),
        ((nx * rows, feats), BF16),
        ((8, nx * rows), F32),
        ((nz, rows, feats), F32),
        ((nz, rows, feats), F32),
        ((nz, rows, feats), F32),
        ((feats, nx * rows), F32),
        ((8, nx * rows), F32),
        ((nx, rows, feats), F32),
        ((2, rows, feats), F32),
        ((2, half, feats), F32),
        ((rows, feats), F32),
        ((rows, feats), F32),
        ((half // 2 + 8, feats), F32),
        ((rows // spread, feats), F32),
        ((rows, feats), BF16),
        ((rows, feats), BF16),
        ((feats, rows), BF16),
        ((feats, rows), BF16),
        ((rows, half), F32),
    ]
    scratch = [pltpu.VMEM(shape, kind) for shape, kind in shapes]
    line = nz * CH
    for count in (2, line, nz, 0, 4, nz, line, 6, 0, CH, spread, spread):
        kind = dma((count,)) if count else dma
        scratch += [kind, kind]
    out = pl.pallas_call(
        functools.partial(kernel, dims),
        out_shape=jax.ShapeDtypeStruct((rows, feats), F32),
        in_specs=[pl.BlockSpec(memory_space=pltpu.VMEM)] * 3,
        out_specs=pl.BlockSpec(memory_space=pltpu.VMEM),
        scratch_shapes=scratch,
        compiler_params=pltpu.CompilerParams(
            collective_id=0, has_side_effects=True, vmem_limit_bytes=56 * 2**20
        ),
    )(particles[0], source_pots, target_pots)
    return out[None]


def solution(mesh):
    times, nx, nz = mesh.shape["tm"], mesh.shape["row"], mesh.shape["col"]

    def program(particles, source_pots, target_pots):
        rows = particles.shape[1] // (nx * nz)
        dims = (times, nx, nz, rows, particles.shape[2])
        return jax.shard_map(
            functools.partial(local, dims),
            mesh=mesh,
            in_specs=(P("tm", ("row", "col"), None), P("tm", ("row", "col")), P("tm", ("row", "col"))),
            out_specs=P("tm", ("row", "col"), None),
            check_vma=False,
        )(particles, source_pots, target_pots)

    return program
```

```python
import functools
import math

import jax
import jax.numpy as jnp
from jax import lax
from jax.experimental import pallas as pl
from jax.experimental.pallas import tpu as pltpu
from jax.sharding import PartitionSpec as P

EPS = 0.1
MESH = pl.DeviceIdType.MESH
F32 = jnp.float32
BF16 = jnp.bfloat16


def split(x):
    hi = x.astype(BF16)
    return hi, (x - hi.astype(F32)).astype(BF16)


def dot(a, b, dims):
    return lax.dot_general(a, b, (dims, ((), ())), preferred_element_type=F32)


def dot3(a, b, dims):
    return dot(a[0], b[0], dims) + dot(a[0], b[1], dims) + dot(a[1], b[0], dims)


def eye(n):
    return lax.broadcasted_iota(jnp.int32, (n, n), 0) == lax.broadcasted_iota(jnp.int32, (n, n), 1)


def to_row(col):
    n = col.shape[0]
    return jnp.sum(jnp.where(eye(n), col, 0.0), axis=0, keepdims=True)


def to_col(row):
    n = row.shape[1]
    return jnp.sum(jnp.where(eye(n), row, 0.0), axis=1, keepdims=True)


BUFS = (
    "sbuf", "mbuf", "mhi", "mlo", "brow", "part", "sib_part", "rsum", "gmt", "csum", "gm",
    "gx_in", "gmid", "gtm_in", "fin", "relay", "back", "shi", "slo", "thi", "tlo", "acol",
)
SEMS = (
    "own", "zr", "sib", "tm", "mx", "pe", "cr", "gx", "gt", "fi",
    "fx", "bx",
)
CH = 4


def kernel(dims, pts_ref, spot_ref, tpot_ref, out_ref, *scratch):
    times, nx, nz, rows, feats = dims
    half = rows // 2
    hrow = half + 8
    piece = rows // CH
    last = nz - 1
    run = nz // 2
    mid = times // 2
    spread = mid // 2
    population = rows * nx * nz
    scale = math.log2(math.e) / EPS
    v = dict(zip(BUFS, scratch))
    sems = {name: scratch[len(BUFS) + 2 * i : len(BUFS) + 2 * i + 2] for i, name in enumerate(SEMS)}
    sbuf, mbuf, part, gm, fin = v["sbuf"], v["mbuf"], v["part"], v["gm"], v["fin"]
    mhi, mlo, brow, gmt, csum = v["mhi"], v["mlo"], v["brow"], v["gmt"], v["csum"]
    gx_in = v["gx_in"]

    tm, x, z = lax.axis_index("tm"), lax.axis_index("row"), lax.axis_index("col")
    core = lax.rem(tm, 2)
    is0, is1 = core == 0, core == 1
    active = tm < times - 1
    cross = tm == mid - 1
    crossed = tm == mid
    fed = jnp.logical_and(jnp.logical_and(is1, active), jnp.logical_not(cross))
    feeds = jnp.logical_and(jnp.logical_and(is0, tm > 0), jnp.logical_not(crossed))
    place = jnp.where(is0, z, last - z)
    has_prev, has_next = place > 0, place < last
    way = 1 - 2 * core
    forth = (tm, x, jnp.clip(z + way, 0, last))
    back_to = (tm, x, jnp.clip(z - way, 0, last))
    sib = (tm + 1 - 2 * core, x, z)
    before, after = (jnp.maximum(tm - 1, 0), x, z), (jnp.minimum(tm + 1, times - 1), x, z)
    x1, x2, x3 = lax.rem(x + 1, nx), lax.rem(x + 2, nx), lax.rem(x + 3, nx)
    xright, xleft = (tm, x1, z), (tm, x3, z)

    def at_time(t):
        return (t, x, z)

    def rdma(src, dst, name, to, k=None):
        s, r = sems[name]
        if k is not None:
            s, r = s.at[k], r.at[k]
        return pltpu.make_async_remote_copy(
            src_ref=src, dst_ref=dst, send_sem=s, recv_sem=r, device_id=to, device_id_type=MESH
        )

    barrier = pltpu.get_barrier_semaphore()

    def greet(to):
        pl.semaphore_signal(barrier, inc=1, device_id=to, device_id_type=MESH)

    for to in (sib, xright, xleft):
        greet(to)
    pl.when(has_prev)(lambda: greet(back_to))
    pl.when(feeds)(lambda: greet(before))
    pl.when(fed)(lambda: greet(after))
    partners = 3 + has_next.astype(jnp.int32)
    partners = partners + feeds.astype(jnp.int32) + fed.astype(jnp.int32)
    far = [mid + 2 * p for p in range(spread)]
    near = [2 * p for p in range(spread)]
    for p in range(spread):
        pl.when(cross)(lambda: greet(at_time(near[p])))
        pl.when(tm == near[p])(lambda: greet(at_time(far[p] if p else mid)))
        if p:
            pl.when(tm == far[p])(lambda: greet(at_time(mid)))

    relaying = jnp.logical_and(is0, jnp.logical_not(crossed))
    partners = partners + jnp.where(crossed, spread, relaying.astype(jnp.int32))

    pts = pts_ref[...]
    norm = to_row(jnp.sum(pts * pts, axis=1, keepdims=True)) * (scale / feats)
    trow = tpot_ref[...] * scale - norm
    srow = spot_ref[...] * scale - norm - math.log2(population)

    def put(buf, b):
        for i in range(2):
            buf[b, i * hrow : i * hrow + half, :] = pts[i * half : (i + 1) * half]
            pair = jnp.concatenate(
                [trow[:, i * half : (i + 1) * half], srow[:, i * half : (i + 1) * half], jnp.zeros((6, half), F32)], axis=0
            )
            buf[b, i * hrow + half : (i + 1) * hrow, :] = jnp.concatenate(
                [pair, jnp.zeros((8, feats - half), F32)], axis=1
            )

    pl.when(is0)(lambda: put(mbuf, x))
    pl.when(is1)(lambda: put(sbuf, z))

    pl.semaphore_wait(barrier, partners)

    def chunk(g, k):
        return pl.ds(pl.multiple_of(g * hrow + k * (half // 2), 8), half // 2 + 8 * k)

    def blk(i):
        return jnp.where(is0, i, last - i)

    def own_copy(i):
        ref = sbuf.at[z, pl.ds(i * hrow, hrow)]
        return rdma(ref, ref, "own", sib, i)

    def tm_copy():
        return rdma(mbuf.at[x], mbuf.at[x], "tm", before)

    h0, h1 = pl.ds(0, hrow), pl.ds(hrow, hrow)

    def mx_send(k):
        if k < 2:
            ref = mbuf.at[x]
        else:
            ref = mbuf.at[x3, h0] if k == 2 else mbuf.at[x1, h1]
        return rdma(ref, ref, "mx", xright if k % 2 == 0 else xleft, k)

    def mx_arrival(k):
        if k < 2:
            ref = mbuf.at[x3] if k == 0 else mbuf.at[x1]
        else:
            ref = mbuf.at[x2, h0] if k == 2 else mbuf.at[x2, h1]
        return rdma(ref, ref, "mx", xright, k)

    pieces = []
    for i in range(2):
        at = i * hrow
        pieces += [(at, half // 2), (at + half // 2, half // 2 + 8)]

    def fx_first(p):
        at, size = pieces[p]
        dst = v["relay"].at[pl.ds(0, size)]
        return rdma(mbuf.at[x, pl.ds(at, size)], dst, "fx", at_time(far[p] if p else near[p]), p)

    def fx_second(p):
        ref = v["relay"].at[pl.ds(0, pieces[p][1])]
        return rdma(ref, ref, "fx", at_time(near[p]), p)

    def fx_third(p):
        at, size = pieces[p]
        src = v["relay"].at[pl.ds(0, size)]
        return rdma(src, mbuf.at[x, pl.ds(at, size)], "fx", at_time(mid - 1), p)

    quarter = rows // spread

    def bx_first(p):
        return rdma(gm.at[x, pl.ds(p * quarter, quarter)], v["back"], "bx", at_time(near[p]), p)

    def bx_second(p):
        dst = v["back"] if p else v["gtm_in"].at[pl.ds(0, quarter)]
        return rdma(v["back"], dst, "bx", at_time(far[p] if p else mid), p)

    def bx_third(p):
        return rdma(v["back"], v["gtm_in"].at[pl.ds(p * quarter, quarter)], "bx", at_time(mid), p)

    def zr_part(s, g, k, b):
        ref = sbuf.at[b, chunk(g, k)]
        return rdma(ref, ref, "zr", forth, s * CH + 2 * g + k)

    def zr_copy(s, c, b):
        return zr_part(s, c // 2, c % 2, b)

    def sib_copy(b):
        return rdma(sbuf.at[b], sbuf.at[b], "sib", sib, b)

    @pl.when(is1)
    def _():
        own_copy(0).start()
        own_copy(1).start()
        for c in range(CH):
            pl.when(has_next)(lambda: zr_copy(0, c, z).start())

    @pl.when(is0)
    def _():
        pl.when(feeds)(lambda: tm_copy().start())

        @pl.when(crossed)
        def _():
            for p in range(spread):
                fx_first(p).start()

        mx_send(0).start()
        mx_send(1).start()
        for i in range(2):
            own_copy(i).wait_recv()
            for c in (2 * i, 2 * i + 1):
                pl.when(has_next)(lambda: zr_copy(0, c, z).start())

    chain_at = nz
    near_at, far_at, back_at = run, 1, 14
    wait_m = jnp.where(cross, run + 1, 1)
    mx_step = jnp.where(cross, run + 2, jnp.where(is0, 2, 3))
    first = jnp.where(cross, nz - 1, jnp.where(is0, 4, 4))
    pace = jnp.where(cross, 2, 1)
    ahead = (nz - first) * pace

    def order(n):
        k = jnp.where(n < ahead, last - n, n - ahead)
        low = jnp.minimum(z, last - z)
        single = last - 2 * low
        d = (k - single) // 2
        b = jnp.where(k < single, last - k, jnp.where(lax.rem(k - single, 2) == 0, 2 * low - d, d))
        return jnp.where(z < nz - nz // 2, b, last - b)

    def pe_copy(b):
        return rdma(part.at[b], v["sib_part"].at[b], "pe", sib, b)

    def prepare():
        mx_arrival(2).wait_recv()
        mx_arrival(3).wait_recv()
        for j in range(nx):
            for i in range(2):
                at = j * rows + i * half
                hi, lo = split(mbuf[j, i * hrow : i * hrow + half, :])
                mhi[at : at + half, :] = hi
                mlo[at : at + half, :] = lo
                pair = mbuf[j, i * hrow + half : (i + 1) * hrow, 0:half]
                brow[0:1, at : at + half] = jnp.where(is0, pair[1:2], pair[0:1])

    def tile_open(b):
        for i in range(2):
            at = slice(i * half, (i + 1) * half)
            s = sbuf[b, i * hrow : i * hrow + half, :]
            hi, lo = split(s)
            v["shi"][at, :] = hi
            v["slo"][at, :] = lo
            hi, lo = split(s.T)
            v["thi"][:, at] = hi
            v["tlo"][:, at] = lo
            pair = sbuf[b, i * hrow + half : (i + 1) * hrow, 0:half]
            v["acol"][at, :] = jnp.broadcast_to(to_col(jnp.where(is0, pair[0:1], pair[1:2])), (half, half))

    def tile_part(b, c):
        width = nx * rows // 2
        at = pl.ds(pl.multiple_of(c * width, width), width)
        m = (mhi[at, :], mlo[at, :])
        g = dot3((v["shi"][...], v["slo"][...]), m, ((1,), (1,)))
        w = jnp.exp2(g * (2.0 * scale / feats) + v["acol"][:, 0:1] + brow[0:1, at])
        total = jnp.sum(w, axis=1, keepdims=True)
        csum[0:1, at] += jnp.sum(w, axis=0, keepdims=True)
        ww = split(w)
        moved = dot3(ww, m, ((1,), (0,)))
        gmt[:, at] += dot3((v["thi"][...], v["tlo"][...]), ww, ((1,), (0,)))
        for i in range(2):
            r = slice(i * half, (i + 1) * half)
            part[b, r, :] = part[b, r, :] + (total[r] * sbuf[b, i * hrow : i * hrow + half, :] - moved[r])

    gmt[...] = jnp.zeros_like(gmt)
    csum[...] = jnp.zeros_like(csum)

    g0, g1 = pl.ds(0, half), pl.ds(half, half)

    def gx_copy(k):
        src, dst = [
            (gm.at[x2, g0], v["gmid"].at[0]),
            (gm.at[x2, g1], v["gmid"].at[1]),
            (gm.at[x1, g1], gx_in.at[0, g1]),
            (gm.at[x3, g0], gx_in.at[1, g0]),
            (gm.at[x1, g0], gx_in.at[0, g0]),
            (gm.at[x3, g1], gx_in.at[1, g1]),
        ][k]
        return rdma(src, dst, "gx", xright if k % 2 == 0 else xleft, k)

    def finish_m(j):
        at = pl.ds(pl.multiple_of(j * rows, rows), rows)
        ccol = to_col(csum[0:1, at])
        g = gmt[:, at].T
        for i in range(2):
            lo = i * half
            gm[j, lo : lo + half, :] = ccol[lo : lo + half] * mbuf[j, i * hrow : i * hrow + half, :] - g[lo : lo + half]

    def gt_copy():
        return rdma(gm.at[x], v["gtm_in"], "gt", after)

    def cr_copy(b, c):
        ref = v["rsum"].at[b, pl.ds(c * piece, piece)]
        return rdma(ref, ref, "cr", forth, b * CH + c)

    def fi_copy(c):
        r = pl.ds(c * piece, piece)
        return rdma(v["rsum"].at[z, r], fin.at[r], "fi", sib, c)

    def step(s, carry):
        @pl.when(jnp.logical_and(is0, s == back_at))
        def _():
            for p in range(spread):

                @pl.when(tm == near[p])
                def _():
                    bx_first(p).wait_recv()
                    bx_second(p).start()

        @pl.when(jnp.logical_and(is0, jnp.logical_or(s == far_at, s == near_at)))
        def _():
            for p in range(1, spread):

                @pl.when(jnp.logical_and(s == far_at, tm == far[p]))
                def _():
                    fx_second(p).wait_recv()
                    fx_second(p).start()

            for p in range(spread):

                @pl.when(jnp.logical_and(s == near_at, tm == near[p]))
                def _():
                    fx_second(p).wait_recv()
                    fx_third(p).start()

        @pl.when(s <= first)
        def _():
            @pl.when(s == wait_m)
            def _():
                @pl.when(fed)
                def _():
                    tm_copy().wait_recv()

                @pl.when(cross)
                def _():
                    for p in range(spread):
                        at, size = pieces[p]
                        ref = mbuf.at[x, pl.ds(at, size)]
                        rdma(ref, ref, "fx", at_time(mid - 1), p).wait_recv()

                @pl.when(jnp.logical_or(fed, cross))
                def _():
                    mx_send(0).start()
                    mx_send(1).start()

            @pl.when(jnp.logical_and(active, s == mx_step))
            def _():
                mx_arrival(0).wait_recv()
                mx_send(2).start()
                mx_arrival(1).wait_recv()
                mx_send(3).start()

            pl.when(jnp.logical_and(active, s == first))(prepare)

        relays = jnp.logical_and(s <= last, s <= place)
        onward = jnp.logical_and(relays, jnp.logical_and(has_next, s < last))
        at = blk(place - s)

        def unit(u, carry):
            c = lax.rem(u, 2)
            n = (s - first) * pace + u // 2
            b = order(jnp.clip(n, 0, last))
            has_tile = jnp.logical_and(n >= 0, n < nz)

            @pl.when(jnp.logical_and(relays, u < 2))
            def _():
                for k in range(2):
                    zr_part(s - 1, u, k, at).wait_recv()
                    pl.when(onward)(lambda: zr_part(s, u, k, at).start())

            @pl.when(has_tile)
            def _():
                @pl.when(c == 0)
                def _():
                    pl.when(jnp.where(is0, b > z, b < z))(lambda: sib_copy(b).wait_recv())
                    part[b] = jnp.zeros((rows, feats), F32)
                    pl.when(active)(lambda: tile_open(b))

                pl.when(active)(lambda: tile_part(b, c))

                @pl.when(jnp.logical_and(c == 1, jnp.where(is0, b <= z, b > z)))
                def _():
                    pe_copy(b).start()

            return carry

        units = jnp.where(jnp.logical_or(s <= last, s < first + nz // pace), 2 * jnp.where(s < first, 1, pace), 0)
        lax.fori_loop(0, units, unit, 0)
        pl.when(relays)(lambda: sib_copy(at).start())

        cs = s - chain_at

        @pl.when(jnp.logical_and(jnp.logical_and(cs >= place, cs < last), has_next))
        def _():
            t = blk(last - cs + place)
            pe_copy(t).wait_recv()
            for c in range(CH):
                r = pl.ds(c * piece, piece)

                @pl.when(has_prev)
                def _():
                    cr_copy(t, c).wait_recv()
                    v["rsum"][t, r, :] = v["rsum"][t, r, :] + (part[t, r, :] + v["sib_part"][t, r, :])

                @pl.when(jnp.logical_not(has_prev))
                def _():
                    v["rsum"][t, r, :] = part[t, r, :] + v["sib_part"][t, r, :]

                cr_copy(t, c).start()

        done = s - first - nz // pace + 1

        @pl.when(jnp.logical_and(active, done >= 0))
        def _():
            @pl.when(done == 0)
            def _():
                finish_m(x2)
                gx_copy(0).start()
                gx_copy(1).start()
                finish_m(x1)
                gx_copy(2).start()
                finish_m(x3)
                gx_copy(3).start()
                finish_m(x)

            @pl.when(done == 1)
            def _():
                gx_copy(0).wait_recv()
                gm[x1, g0, :] = gm[x1, g0, :] + v["gmid"][0]
                gx_copy(4).start()
                gx_copy(1).wait_recv()
                gm[x3, g1, :] = gm[x3, g1, :] + v["gmid"][1]
                gx_copy(5).start()

            @pl.when(done == 2)
            def _():
                for k in range(2, 6):
                    gx_copy(k).wait_recv()
                gm[x] = gm[x] + gx_in[0] + gx_in[1]
                pl.when(fed)(lambda: gt_copy().start())

                @pl.when(cross)
                def _():
                    for p in range(spread):
                        bx_first(p).start()

        return carry

    steps = jnp.maximum(first + nz // pace + 3, chain_at + last)
    lax.fori_loop(1, steps, step, 0)

    @pl.when(is0)
    def _():
        @pl.when(has_prev)
        def _():
            for c in range(CH):
                cr_copy(z, c).wait_recv()
                fi_copy(c).start()

        out_ref[...] = gm[x]

        @pl.when(feeds)
        def _():
            gt_copy().wait_recv()
            out_ref[...] = out_ref[...] + v["gtm_in"][...]

    for p in range(1, spread):

        @pl.when(tm == far[p])
        def _():
            bx_second(p).wait_recv()
            bx_third(p).start()

    @pl.when(crossed)
    def _():
        for p in range(spread):
            bx_third(p).wait_recv()
        out_ref[...] = out_ref[...] + v["gtm_in"][...]

    @pl.when(is1)
    def _():
        pe_copy(z).wait_recv()
        out_ref[...] = part[z] + v["sib_part"][z]
        for c in range(CH):
            r = pl.ds(c * piece, piece)

            @pl.when(has_prev)
            def _():
                cr_copy(z, c).wait_recv()
                out_ref[r, :] = out_ref[r, :] + v["rsum"][z, r, :]

            @pl.when(z > 0)
            def _():
                fi_copy(c).wait_recv()
                out_ref[r, :] = out_ref[r, :] + fin[r, :]

    @pl.when(is1)
    def _():
        own_copy(0).wait_send()
        own_copy(1).wait_send()

    @pl.when(jnp.logical_and(is0, has_prev))
    def _():
        for c in range(CH):
            fi_copy(c).wait_send()

    pl.when(feeds)(lambda: tm_copy().wait_send())
    pl.when(fed)(lambda: gt_copy().wait_send())
    for p in range(spread):

        @pl.when(crossed)
        def _():
            fx_first(p).wait_send()

        @pl.when(cross)
        def _():
            bx_first(p).wait_send()

        @pl.when(tm == near[p])
        def _():
            fx_third(p).wait_send()
            bx_second(p).wait_send()

        if p:

            @pl.when(tm == far[p])
            def _():
                fx_second(p).wait_send()
                bx_third(p).wait_send()

    @pl.when(active)
    def _():
        for k in range(4):
            mx_send(k).wait_send()
        for k in range(6):
            gx_copy(k).wait_send()

    def drain(i, carry):
        b = blk(i)
        pl.when(jnp.where(is0, b <= z, b > z))(lambda: pe_copy(b).wait_send())
        pl.when(i < place)(lambda: sib_copy(b).wait_send())
        for c in range(CH):
            pl.when(jnp.logical_and(has_next, i <= place))(lambda: zr_copy(place - i, c, b).wait_send())
            pl.when(i > place)(lambda: cr_copy(b, c).wait_send())
        return carry

    lax.fori_loop(0, nz, drain, 0)


def local(dims, particles, source_pots, target_pots):
    times, nx, nz, rows, feats = dims
    half = rows // 2
    spread = times // 4
    dma = pltpu.SemaphoreType.DMA
    shapes = [
        ((nz, rows + 16, feats), F32),
        ((nx, rows + 16, feats), F32),
        ((nx * rows, feats), BF16),
        ((nx * rows, feats), BF16),
        ((8, nx * rows), F32),
        ((nz, rows, feats), F32),
        ((nz, rows, feats), F32),
        ((nz, rows, feats), F32),
        ((feats, nx * rows), F32),
        ((8, nx * rows), F32),
        ((nx, rows, feats), F32),
        ((2, rows, feats), F32),
        ((2, half, feats), F32),
        ((rows, feats), F32),
        ((rows, feats), F32),
        ((half // 2 + 8, feats), F32),
        ((rows // spread, feats), F32),
        ((rows, feats), BF16),
        ((rows, feats), BF16),
        ((feats, rows), BF16),
        ((feats, rows), BF16),
        ((rows, half), F32),
    ]
    scratch = [pltpu.VMEM(shape, kind) for shape, kind in shapes]
    line = nz * CH
    for count in (2, line, nz, 0, 4, nz, line, 6, 0, CH, spread, spread):
        kind = dma((count,)) if count else dma
        scratch += [kind, kind]
    out = pl.pallas_call(
        functools.partial(kernel, dims),
        out_shape=jax.ShapeDtypeStruct((rows, feats), F32),
        in_specs=[pl.BlockSpec(memory_space=pltpu.VMEM)] * 3,
        out_specs=pl.BlockSpec(memory_space=pltpu.VMEM),
        scratch_shapes=scratch,
        compiler_params=pltpu.CompilerParams(
            collective_id=0, has_side_effects=True, vmem_limit_bytes=56 * 2**20
        ),
    )(particles[0], source_pots, target_pots)
    return out[None]


def solution(mesh):
    times, nx, nz = mesh.shape["tm"], mesh.shape["row"], mesh.shape["col"]

    def program(particles, source_pots, target_pots):
        rows = particles.shape[1] // (nx * nz)
        dims = (times, nx, nz, rows, particles.shape[2])
        return jax.shard_map(
            functools.partial(local, dims),
            mesh=mesh,
            in_specs=(P("tm", ("row", "col"), None), P("tm", ("row", "col")), P("tm", ("row", "col"))),
            out_specs=P("tm", ("row", "col"), None),
            check_vma=False,
        )(particles, source_pots, target_pots)

    return program
```
